32 devices in a mesh: src: 4 (over y, x), rcv: 8 (over z, core).
Axes of the slice: x: 2, y: 2, z: 4, core: 2. Of those that a mesh axis runs over, the one named last changes fastest.
Arguments:
- record: bfloat16 [1, 2, 6144, 6144], P(None, None, 'rcv', 'src'), may hold values from -6 to 6
- panel_offset: int32 [768], replicated, may hold values from 0 to 7
Outputs:
- primaries: bfloat16 [1, 2, 6144, 6144], P(None, None, 'rcv', 'src')
- multiples: bfloat16 [1, 2, 6144, 6144], P(None, None, 'rcv', 'src')
The draws below stay inside these ranges and needn't reach their ends.
Inputs may be any that keep to these rules, and one draw needn't show every extreme that they name: Panel station j is 8 * j + panel_offset[j].
All inputs are finite; a program needn't handle non-finite values.
Results may differ from the reference program's by a relative error of at most 0.003.
The reference program's roundings to bfloat16 on the way count: a program that leaves them out, or rounds other values in their place, can miss the bound.
Values may be sent and summed in bfloat16 or wider, within the bound.
A program may use at most 128 MiB of HBM per device.

```python
import jax
import jax.numpy as jnp
from jax import lax

NFREQ = 1
NSTA = 6144
STRIDE = 8
REACH = 4
SWEEPS = 2
PANEL = 768
N_SRC = 4
N_RCV = 8


def with_ends(entries, key, least, largest):
    spot = [jax.random.randint(jax.random.fold_in(key, axis), (), 0, length) for axis, length in enumerate(entries.shape)]
    longest = entries.shape.index(max(entries.shape))
    neighbour = spot[:longest] + [(spot[longest] + 1) % entries.shape[longest]] + spot[longest + 1:]
    return entries.at[tuple(spot)].set(least).at[tuple(neighbour)].set(largest)


def level_of(stream_key, extent, split, smallest, largest):
    gain, own = 1.0, jax.random.fold_in(stream_key, 6)
    for position, shards_of in split:
        draws = jnp.exp(jax.random.uniform(jax.random.fold_in(own, position), (shards_of,), jnp.float32, smallest / len(split), largest / len(split)))
        gain = gain * jnp.repeat(draws, extent[position] // shards_of).reshape([-1 if axis == position else 1 for axis in range(len(extent))])
    return gain


def normal_values(rng, dims, scale, limit, pieces=(), kind=jnp.bfloat16):
    result = jax.random.normal(rng, dims, jnp.float32) * scale
    if len(pieces) > 0:
        result = level_of(rng, dims, pieces, -0.22, 0.18) * result
    return jnp.clip(result, min=-limit, max=limit).astype(kind)


def setup_inputs(seed: int = 0) -> dict:
    arg_keys = jax.random.split(jax.random.key(seed), 3)
    return {
        "record": normal_values(arg_keys[0], (NFREQ, 2, NSTA, NSTA), 1.0, 6.0, ((2, 8), (3, 4))),
        "panel_offset": with_ends(jax.random.randint(arg_keys[1], (PANEL,), 0, STRIDE), jax.random.fold_in(arg_keys[1], 1), 0, STRIDE - 1).astype(jnp.int32),
    }


weight_eps = 1e-6


def box_total(values):
    rows_recv = values.shape[0]
    rows_source = values.shape[1]
    padded = jnp.pad(values, ((REACH, REACH), (REACH, REACH)))
    recv_total = padded[0:rows_recv, :]
    for shift_pos in range(1, 2 * REACH + 1):
        recv_total = recv_total + padded[shift_pos:shift_pos + rows_recv, :]
    box_totals = recv_total[:, 0:rows_source]
    for shift_pos in range(1, 2 * REACH + 1):
        box_totals = box_totals + recv_total[:, shift_pos:shift_pos + rows_source]
    return box_totals


def reference(record, panel_offset):
    stations = record.shape[2]
    src_rows = stations // N_SRC
    rcv_cols = stations // N_RCV
    run_len = stations // (N_SRC * N_RCV)
    station = jnp.arange(stations, dtype=jnp.int32)
    column_of = rcv_cols * ((station % src_rows) // run_len) + run_len * (station // src_rows) + station % run_len
    station_of = src_rows * ((station % rcv_cols) // run_len) + run_len * (station // rcv_cols) + station % run_len
    natural = jnp.take(record, column_of.astype(jnp.int32), axis=2)
    keys = (STRIDE * jnp.arange(PANEL, dtype=jnp.int32) + panel_offset).astype(jnp.int32)
    front = jnp.swapaxes(jnp.take(natural, keys, axis=2), 2, 3)
    behind = jnp.take(natural, keys, axis=3)
    symmetric = ((front.astype(jnp.float32) + behind.astype(jnp.float32)) * 0.5).astype(jnp.bfloat16)
    prim_list = []
    mult_list = []
    for freq_index in range(NFREQ):
        real_part = symmetric[freq_index, 0]
        imag_part = symmetric[freq_index, 1]
        pred_real = jnp.dot(real_part, real_part.T, preferred_element_type=jnp.float32) - jnp.dot(imag_part, imag_part.T, preferred_element_type=jnp.float32)
        pred_imag = jnp.dot(real_part, imag_part.T, preferred_element_type=jnp.float32) + jnp.dot(imag_part, real_part.T, preferred_element_type=jnp.float32)
        round_real = lax.optimization_barrier(pred_real.astype(jnp.bfloat16)).astype(jnp.float32)
        round_imag = lax.optimization_barrier(pred_imag.astype(jnp.bfloat16)).astype(jnp.float32)
        data_real = natural[freq_index, 0].astype(jnp.float32)
        data_imag = natural[freq_index, 1].astype(jnp.float32)
        err_real = data_real
        err_imag = data_imag
        for sweep_step in range(SWEEPS):
            weight = 1.5 - jnp.tanh(err_real * err_real + err_imag * err_imag)
            num_real = box_total(weight * (round_real * data_real + round_imag * data_imag))
            num_imag = box_total(weight * (round_real * data_imag - round_imag * data_real))
            denom = box_total(weight * (round_real * round_real + round_imag * round_imag)) + weight_eps
            gain_real = num_real / denom
            gain_imag = num_imag / denom
            err_real = data_real - (gain_real * round_real - gain_imag * round_imag)
            err_imag = data_imag - (gain_real * round_imag + gain_imag * round_real)
        prim_list.append(jnp.stack([err_real, err_imag]))
        mult_list.append(jnp.stack([pred_real, pred_imag]) * (PANEL ** -0.5))
    primaries = jnp.take(jnp.stack(prim_list), station_of.astype(jnp.int32), axis=2).astype(jnp.bfloat16)
    multiples = jnp.take(jnp.stack(mult_list), station_of.astype(jnp.int32), axis=2).astype(jnp.bfloat16)
    return primaries, multiples
```

```python
import functools

import jax
import jax.numpy as jnp
from jax import lax
from jax.experimental import pallas as pl
from jax.experimental.pallas import tpu as pltpu
from jax.sharding import PartitionSpec as P

STRIDE = 8
REACH = 4
SWEEPS = 2


weight_eps = 1e-06


def extended(cells, sides, width, closed):
    for axis, dim in sides:
        count = lax.axis_size(axis)
        ends = count if closed else count - 1
        head = lax.slice_in_dim(cells, 0, width, axis=dim)
        tail = lax.slice_in_dim(cells, cells.shape[dim] - width, cells.shape[dim], axis=dim)
        cells = jnp.concatenate(
            [
                lax.ppermute(tail, axis, [(i, (i + 1) % count) for i in range(ends)]),
                cells,
                lax.ppermute(head, axis, [((i + 1) % count, i) for i in range(ends)]),
            ],
            axis=dim,
        )
    return cells


def reorder_keys(values, rcv_count, src_count):
    full_shape = values.shape
    grouped = values.reshape(
        full_shape[:-1] + (rcv_count, src_count, full_shape[-1] // (rcv_count * src_count))
    )
    return jnp.swapaxes(grouped, -3, -2).reshape(full_shape)


def average_pair(first_part, second_part):
    return ((first_part.astype(jnp.float32) + second_part.astype(jnp.float32)) * 0.5).astype(
        jnp.bfloat16
    )


def cross_dot(left_mat, right_mat):
    return lax.dot_general(
        left_mat, right_mat, (((2,), (2,)), ((0,), (0,))), preferred_element_type=jnp.float32
    )


def predict_block(right_side, left_side):
    right_real = right_side[:, 0]
    right_imag = right_side[:, 1]
    left_real = left_side[:, 0]
    left_imag = left_side[:, 1]
    pred_real = cross_dot(right_real, left_real) - cross_dot(right_imag, left_imag)
    pred_imag = cross_dot(right_real, left_imag) + cross_dot(right_imag, left_real)
    return jnp.stack([pred_real, pred_imag], axis=1)


def neighbour_sum(partial_terms, src_count, rcv_pos, rcv_count):
    freq_count, chan_count, rcv_cols, src_rows = partial_terms.shape
    run_len = rcv_cols // src_count
    runs_view = partial_terms.reshape(freq_count, chan_count, src_count, run_len, src_rows)
    padded = extended(runs_view.astype(jnp.bfloat16), (("rcv", 3),), REACH, True).astype(
        runs_view.dtype
    )
    lower_rim = padded[:, :, :, :REACH]
    middle = padded[:, :, :, REACH : REACH + run_len]
    upper_rim = padded[:, :, :, REACH + run_len :]
    zero_rim = jnp.zeros_like(lower_rim[:, :, :1])
    lower_rim = jnp.where(
        rcv_pos == 0, jnp.concatenate([zero_rim, lower_rim[:, :, :-1]], axis=2), lower_rim
    )
    upper_rim = jnp.where(
        rcv_pos == rcv_count - 1,
        jnp.concatenate([upper_rim[:, :, 1:], zero_rim], axis=2),
        upper_rim,
    )
    padded = jnp.concatenate([lower_rim, middle, upper_rim], axis=3)
    recv_total = padded[:, :, :, 0:run_len]
    for shift_pos in range(1, 2 * REACH + 1):
        recv_total = recv_total + padded[:, :, :, shift_pos : shift_pos + run_len]
    recv_total = recv_total.reshape(freq_count, chan_count, rcv_cols, src_rows)
    src_padded = extended(recv_total.astype(jnp.bfloat16), (("src", 3),), REACH, False).astype(
        recv_total.dtype
    )
    box_totals = src_padded[..., 0:src_rows]
    for shift_pos in range(1, 2 * REACH + 1):
        box_totals = box_totals + src_padded[..., shift_pos : shift_pos + src_rows]
    return box_totals


def run_sweeps(data_bf, pred_bf, summer):
    data_f32 = data_bf.astype(jnp.float32)
    pred_f32 = pred_bf.astype(jnp.float32)
    data_real = data_f32[:, 0]
    data_imag = data_f32[:, 1]
    pred_real = pred_f32[:, 0]
    pred_imag = pred_f32[:, 1]
    err_real = data_real
    err_imag = data_imag
    for sweep_step in range(SWEEPS):
        weight = 1.5 - jnp.tanh(err_real * err_real + err_imag * err_imag)
        partial_terms = jnp.stack(
            [
                weight * (pred_real * data_real + pred_imag * data_imag),
                weight * (pred_real * data_imag - pred_imag * data_real),
                weight * (pred_real * pred_real + pred_imag * pred_imag),
            ],
            axis=1,
        )
        box_totals = summer(partial_terms)
        denom = box_totals[:, 2] + weight_eps
        gain_real = box_totals[:, 0] / denom
        gain_imag = box_totals[:, 1] / denom
        err_real = data_real - (gain_real * pred_real - gain_imag * pred_imag)
        err_imag = data_imag - (gain_real * pred_imag + gain_imag * pred_real)
    return jnp.stack([err_real, err_imag], axis=1)


def plain_shards(record, panel_offset):
    src_count = lax.axis_size("src")
    rcv_count = lax.axis_size("rcv")
    src_pos = lax.axis_index("src")
    rcv_pos = lax.axis_index("rcv")
    rcv_cols = record.shape[2]
    src_rows = record.shape[3]
    run_len = rcv_cols // src_count
    per_run = run_len // STRIDE
    panel_len = panel_offset.shape[0]
    run_ids = jnp.arange(src_count, dtype=jnp.int32)[:, None]
    within = jnp.arange(per_run, dtype=jnp.int32)[None, :]
    col_groups = (src_rows * run_ids + run_len * rcv_pos) // STRIDE + within
    col_index = (run_len * run_ids + STRIDE * within + jnp.take(panel_offset, col_groups)).reshape(
        -1
    )
    row_groups = jnp.arange(src_rows // STRIDE, dtype=jnp.int32)
    row_index = STRIDE * row_groups + jnp.take(
        panel_offset, src_rows // STRIDE * src_pos + row_groups
    )
    col_piece = jnp.swapaxes(jnp.take(record, col_index, axis=2), 2, 3)
    row_piece = jnp.take(record, row_index, axis=3)
    own_front = reorder_keys(
        lax.all_to_all(col_piece, "rcv", split_axis=2, concat_axis=3, tiled=True),
        rcv_count,
        src_count,
    )
    own_behind = lax.all_to_all(row_piece, "src", split_axis=2, concat_axis=3, tiled=True)
    owned_rows = average_pair(own_front, own_behind)
    right_side = lax.all_gather(owned_rows, "src", axis=2, tiled=True)
    prediction = predict_block(right_side, lax.all_gather(owned_rows, "rcv", axis=2, tiled=True))
    pred_round = lax.optimization_barrier(prediction.astype(jnp.bfloat16))
    multiples = (prediction * panel_len ** (-0.5)).astype(jnp.bfloat16)

    def runs_total(partial_terms):
        return neighbour_sum(partial_terms, src_count, rcv_pos, rcv_count)

    primaries = run_sweeps(record, pred_round, runs_total).astype(jnp.bfloat16)
    return (primaries, multiples)

HALO = 2 * REACH


def wide_spans(width):
    spans = [(start, 256) for start in range(0, width - 255, 256)]
    done = 256 * (width // 256)
    return spans + ([(done, width - done)] if done < width else [])


def band(shape, shift, period):
    rows = lax.broadcasted_iota(jnp.int32, shape, 0)
    cols = lax.broadcasted_iota(jnp.int32, shape, 1) + shift
    gap = jnp.abs(rows - cols)
    if period:
        gap = jnp.minimum(gap, period - gap)
    return jnp.where(gap <= REACH, 1.0, 0.0).astype(jnp.bfloat16)


def sweep_kernel(
    scale, record_ref, rim_ref, side_ref, right_ref, left_ref, prim_ref, mult_ref,
    left_all, right_all, data, pred32, predb, terms, partial, totals, row_band, lane_band
):
    runs_len = record_ref.shape[2]
    src_rows = record_ref.shape[3]
    owners = left_ref.shape[0]
    rows = runs_len + 2 * HALO
    width = src_rows + 128
    panel = left_ref.shape[3]
    f32, bf = jnp.float32, jnp.bfloat16

    @pl.when(pl.program_id(0) == 0)
    def _():
        row_band[...] = band((rows, rows), 0, rows)
        lane_band[...] = band((512, 256), 128, 0)
        left_all[src_rows:, :] = jnp.zeros((128, 2 * panel), bf)
        for chan in range(2):
            lanes = slice(chan * panel, (chan + 1) * panel)
            for owner in range(owners):
                left_all[owner * runs_len : (owner + 1) * runs_len, lanes] = left_ref[
                    owner, chan, :runs_len
                ]
            after = left_ref[owners - 1, chan, runs_len:]
            before = left_ref[0, chan, runs_len:]
            spot = lax.broadcasted_iota(jnp.int32, after.shape, 0)
            zero = jnp.zeros_like(after)
            left_all[src_rows : src_rows + 2 * HALO, lanes] = jnp.where(spot < HALO, after, zero)
            left_all[width - 2 * HALO : width, lanes] = jnp.where(spot >= HALO, before, zero)

    for chan in range(2):
        data[chan, :runs_len, :src_rows] = record_ref[0, chan]
        data[chan, runs_len:, :src_rows] = rim_ref[chan, 0]
        data[chan, :, src_rows:] = side_ref[chan, 0]
    right_real = right_ref[0, 0]
    right_imag = right_ref[0, 1]
    right_all[:rows, :panel] = right_real
    right_all[:rows, panel:] = -right_imag
    right_all[rows:, :panel] = right_imag
    right_all[rows:, panel:] = right_real
    for start, size in wide_spans(width):
        pred32[:, start : start + size] = lax.dot_general(
            right_all[...],
            left_all[start : start + size, :],
            (((1,), (1,)), ((), ())),
            preferred_element_type=f32,
        )

    def put_terms(at, lanes, err, here, guess):
        weight = 1.5 - jnp.tanh(err[0] * err[0] + err[1] * err[1])
        parts = (
            guess[0] * here[0] + guess[1] * here[1],
            guess[0] * here[1] - guess[1] * here[0],
            guess[0] * guess[0] + guess[1] * guess[1],
        )
        for index, part in enumerate(parts):
            terms[index, at, lanes] = (weight * part).astype(bf)

    def new_err(at, lanes):
        here = [data[chan, at, lanes].astype(f32) for chan in range(2)]
        guess = [predb[chan, at, lanes].astype(f32) for chan in range(2)]
        inverse = 1.0 / (totals[2, at, lanes] + weight_eps)
        gain_real = totals[0, at, lanes] * inverse
        gain_imag = totals[1, at, lanes] * inverse
        err = (
            here[0] - (gain_real * guess[0] - gain_imag * guess[1]),
            here[1] - (gain_real * guess[1] + gain_imag * guess[0]),
        )
        return err, here, guess

    def box():
        for index in range(3):
            for start, size in wide_spans(width):
                partial[index, :, 128 + start : 128 + start + size] = jnp.dot(
                    row_band[...], terms[index, :, start : start + size], preferred_element_type=f32
                ).astype(bf)
            partial[index, :, :128] = partial[index, :, width : width + 128]
            partial[index, :, width + 128 :] = partial[index, :, 128:256]
        for index in range(3):
            for start, size in wide_spans(width):
                totals[index, :, start : start + size] = jnp.dot(
                    partial[index, :, start : start + size + 256],
                    lane_band[: size + 256, :size],
                    preferred_element_type=f32,
                )

    @pl.loop(0, rows // 16)
    def _(step):
        at = pl.ds(pl.multiple_of(step * 16, 16), 16)
        at_imag = pl.ds(pl.multiple_of(rows + step * 16, 16), 16)
        for block in range(width // 128):
            lanes = slice(block * 128, (block + 1) * 128)
            here = [data[chan, at, lanes].astype(f32) for chan in range(2)]
            guess = []
            for chan, spot in enumerate((at, at_imag)):
                rounded = pred32[spot, lanes].astype(bf)
                predb[chan, at, lanes] = rounded
                guess.append(rounded.astype(f32))
            put_terms(at, lanes, here, here, guess)

    @pl.loop(0, runs_len // 16)
    def _(step):
        at = pl.ds(pl.multiple_of(step * 16, 16), 16)
        at_imag = pl.ds(pl.multiple_of(rows + step * 16, 16), 16)
        for block in range(src_rows // 128):
            lanes = slice(block * 128, (block + 1) * 128)
            mult_ref[0, 0, at, lanes] = (pred32[at, lanes] * scale).astype(bf)
            mult_ref[0, 1, at, lanes] = (pred32[at_imag, lanes] * scale).astype(bf)

    for sweep_step in range(SWEEPS - 1):
        box()

        @pl.loop(0, rows // 16)
        def _(step):
            at = pl.ds(pl.multiple_of(step * 16, 16), 16)
            for block in range(width // 128):
                lanes = slice(block * 128, (block + 1) * 128)
                put_terms(at, lanes, *new_err(at, lanes))

    box()

    @pl.loop(0, runs_len // 16)
    def _(step):
        at = pl.ds(pl.multiple_of(step * 16, 16), 16)
        for block in range(src_rows // 128):
            lanes = slice(block * 128, (block + 1) * 128)
            err, _, _ = new_err(at, lanes)
            prim_ref[0, 0, at, lanes] = err[0].astype(bf)
            prim_ref[0, 1, at, lanes] = err[1].astype(bf)


def sweep_call(record, rims, sides, right, left):
    _, _, rcv_cols, src_rows = record.shape
    runs = right.shape[0]
    run_len = rcv_cols // runs
    rows = run_len + 2 * HALO
    width = src_rows + 128
    panel = left.shape[3]
    f32, bf = jnp.float32, jnp.bfloat16
    out = jax.ShapeDtypeStruct(record.shape, bf)
    tile = pl.BlockSpec((1, 2, run_len, src_rows), lambda r: (0, 0, r, 0))
    return pl.pallas_call(
        functools.partial(sweep_kernel, panel ** (-0.5)),
        grid=(runs,),
        out_shape=(out, out),
        in_specs=[
            tile,
            pl.BlockSpec((2, 1, 2 * HALO, src_rows), lambda r: (0, r, 0, 0)),
            pl.BlockSpec((2, 1, rows, 128), lambda r: (0, r, 0, 0)),
            pl.BlockSpec((1, 2, rows, panel), lambda r: (r, 0, 0, 0)),
            pl.BlockSpec(left.shape, lambda r: (0, 0, 0, 0), pipeline_mode=pl.Buffered(1)),
        ],
        out_specs=(tile, tile),
        scratch_shapes=[
            pltpu.VMEM((width, 2 * panel), bf),
            pltpu.VMEM((2 * rows, 2 * panel), bf),
            pltpu.VMEM((2, rows, width), bf),
            pltpu.VMEM((2 * rows, width), f32),
            pltpu.VMEM((2, rows, width), bf),
            pltpu.VMEM((3, rows, width), bf),
            pltpu.VMEM((3, rows, width + 256), bf),
            pltpu.VMEM((3, rows, width), f32),
            pltpu.VMEM((rows, rows), bf),
            pltpu.VMEM((512, 256), bf),
        ],
        compiler_params=pltpu.CompilerParams(vmem_limit_bytes=56 * 1024 * 1024),
        cost_estimate=pl.CostEstimate(
            flops=20_000_000_000, bytes_accessed=4 * record.size * 2, transcendentals=2 * record.size
        ),
    )(record, rims, sides, right, left)


def average_kernel(front_ref, behind_ref, own_ref):
    srcs = behind_ref.shape[1]
    rcvs = front_ref.shape[1]
    panel = own_ref.shape[2]
    each = panel // (srcs * rcvs)
    f32, bf = jnp.float32, jnp.bfloat16

    for chan in range(2):
        total = jnp.zeros(own_ref.shape[1:], f32)
        for rcv in range(rcvs):
            shape = (srcs * each, panel)
            index = lax.broadcasted_iota(jnp.int32, shape, 0)
            column = lax.broadcasted_iota(jnp.int32, shape, 1)
            aim = index // each * (rcvs * each) + rcv * each + index % each
            pick = jnp.where(column == aim, 1.0, 0.0).astype(bf)
            total = total + jnp.dot(front_ref[chan, rcv], pick, preferred_element_type=f32)
        for src in range(srcs):
            shape = (rcvs * each, panel)
            index = lax.broadcasted_iota(jnp.int32, shape, 0)
            column = lax.broadcasted_iota(jnp.int32, shape, 1)
            pick = jnp.where(column == index + src * rcvs * each, 1.0, 0.0).astype(bf)
            total = total + jnp.dot(behind_ref[chan, src], pick, preferred_element_type=f32)
        own_ref[chan] = (total * 0.5).astype(bf)


def average_call(front, behind, panel):
    return pl.pallas_call(
        average_kernel,
        out_shape=jax.ShapeDtypeStruct((2, front.shape[2], panel), jnp.bfloat16),
        in_specs=[pl.BlockSpec(memory_space=pltpu.VMEM)] * 2,
        out_specs=pl.BlockSpec(memory_space=pltpu.VMEM),
        compiler_params=pltpu.CompilerParams(vmem_limit_bytes=32 * 1024 * 1024),
    )(front, behind)


def panel_places(panel_offset, src_count, rcv_count, src_pos, rcv_pos, run_len, src_rows):
    per_run = run_len // STRIDE
    run_ids = jnp.arange(src_count, dtype=jnp.int32)[:, None]
    within = jnp.arange(per_run, dtype=jnp.int32)[None, :]
    by_block = panel_offset.reshape(src_count, rcv_count, per_run)
    mine = lax.dynamic_index_in_dim(by_block, rcv_pos, axis=1, keepdims=False)
    col_index = (run_len * run_ids + STRIDE * within + mine).reshape(-1)
    groups = jnp.arange(src_rows // STRIDE, dtype=jnp.int32)
    row_index = STRIDE * groups + lax.dynamic_index_in_dim(
        panel_offset.reshape(src_count, -1), src_pos, axis=0, keepdims=False
    )
    return col_index, row_index


def record_rims(rec, src_count, rcv_count, rcv_pos):
    ring = [(i, (i + 1) % rcv_count) for i in range(rcv_count)]
    back = [(b, a) for a, b in ring]
    below = lax.ppermute(rec[:, :, :HALO], "rcv", back)
    above = lax.ppermute(rec[:, :, -HALO:], "rcv", ring)
    zero = jnp.zeros_like(below[:, :1])
    below = jnp.where(
        rcv_pos == rcv_count - 1, jnp.concatenate([below[:, 1:], zero], axis=1), below
    )
    above = jnp.where(rcv_pos == 0, jnp.concatenate([zero, above[:, :-1]], axis=1), above)
    rims = jnp.concatenate([below, above], axis=2)
    head = jnp.concatenate([rec[..., :HALO], rims[..., :HALO]], axis=2)
    tail = jnp.concatenate([rec[..., -HALO:], rims[..., -HALO:]], axis=2)
    line = [(i, i + 1) for i in range(src_count - 1)]
    after = lax.ppermute(head, "src", [(b, a) for a, b in line])
    before = lax.ppermute(tail, "src", line)
    gap = jnp.zeros(after.shape[:-1] + (128 - 2 * HALO,), after.dtype)
    return rims, jnp.concatenate([after, gap, before], axis=-1)


def shards(record, panel_offset):
    src_count = lax.axis_size("src")
    rcv_count = lax.axis_size("rcv")
    freqs, _, rcv_cols, src_rows = record.shape
    run_len = rcv_cols // src_count
    if freqs != 1 or run_len % 16 or src_rows % 128:
        return plain_shards(record, panel_offset)
    src_pos = lax.axis_index("src")
    rcv_pos = lax.axis_index("rcv")
    panel = panel_offset.shape[0]
    col_index, row_index = panel_places(
        panel_offset, src_count, rcv_count, src_pos, rcv_pos, run_len, src_rows
    )
    rec = record[0]
    col_pick = (jnp.arange(rcv_cols)[:, None] == col_index[None, :]).astype(record.dtype)
    row_pick = (jnp.arange(src_rows)[:, None] == row_index[None, :]).astype(record.dtype)
    front = lax.dot_general(
        rec, col_pick, (((1,), (0,)), ((), ())), preferred_element_type=jnp.float32
    ).astype(record.dtype)
    behind = lax.dot_general(
        rec, row_pick, (((2,), (0,)), ((), ())), preferred_element_type=jnp.float32
    ).astype(record.dtype)
    front = lax.all_to_all(
        front.reshape(2, rcv_count, run_len, -1), "rcv", split_axis=1, concat_axis=1, tiled=True
    )
    behind = lax.all_to_all(
        behind.reshape(2, src_count, run_len, -1), "src", split_axis=1, concat_axis=1, tiled=True
    )
    own = average_call(front, behind, panel)
    total = src_count * rcv_count
    line = [(i, i + 1) for i in range(total - 1)]
    below = lax.ppermute(own[:, :HALO], ("src", "rcv"), [(b, a) for a, b in line])
    above = lax.ppermute(own[:, -HALO:], ("src", "rcv"), line)
    own = jnp.concatenate([own, below, above], axis=1)
    right = lax.all_gather(own, "src", axis=0)
    left = lax.all_gather(own, "rcv", axis=0)
    rims, sides = record_rims(
        rec.reshape(2, src_count, run_len, src_rows), src_count, rcv_count, rcv_pos
    )
    return sweep_call(record, rims, sides, right, left)


def solution(mesh):
    in_specs = (P(None, None, "rcv", "src"), P())
    out_specs = (P(None, None, "rcv", "src"), P(None, None, "rcv", "src"))
    return jax.shard_map(shards, mesh=mesh, in_specs=in_specs, out_specs=out_specs, check_vma=False)
```

```python
import functools

import jax
import jax.numpy as jnp
from jax import lax
from jax.experimental import pallas as pl
from jax.experimental.pallas import tpu as pltpu
from jax.sharding import PartitionSpec as P

STRIDE = 8
REACH = 4
SWEEPS = 2


weight_eps = 1e-06


def extended(cells, sides, width, closed):
    for axis, dim in sides:
        count = lax.axis_size(axis)
        ends = count if closed else count - 1
        head = lax.slice_in_dim(cells, 0, width, axis=dim)
        tail = lax.slice_in_dim(cells, cells.shape[dim] - width, cells.shape[dim], axis=dim)
        cells = jnp.concatenate(
            [
                lax.ppermute(tail, axis, [(i, (i + 1) % count) for i in range(ends)]),
                cells,
                lax.ppermute(head, axis, [((i + 1) % count, i) for i in range(ends)]),
            ],
            axis=dim,
        )
    return cells


def reorder_keys(values, rcv_count, src_count):
    full_shape = values.shape
    grouped = values.reshape(
        full_shape[:-1] + (rcv_count, src_count, full_shape[-1] // (rcv_count * src_count))
    )
    return jnp.swapaxes(grouped, -3, -2).reshape(full_shape)


def average_pair(first_part, second_part):
    return ((first_part.astype(jnp.float32) + second_part.astype(jnp.float32)) * 0.5).astype(
        jnp.bfloat16
    )


def cross_dot(left_mat, right_mat):
    return lax.dot_general(
        left_mat, right_mat, (((2,), (2,)), ((0,), (0,))), preferred_element_type=jnp.float32
    )


def predict_block(right_side, left_side):
    right_real = right_side[:, 0]
    right_imag = right_side[:, 1]
    left_real = left_side[:, 0]
    left_imag = left_side[:, 1]
    pred_real = cross_dot(right_real, left_real) - cross_dot(right_imag, left_imag)
    pred_imag = cross_dot(right_real, left_imag) + cross_dot(right_imag, left_real)
    return jnp.stack([pred_real, pred_imag], axis=1)


def neighbour_sum(partial_terms, src_count, rcv_pos, rcv_count):
    freq_count, chan_count, rcv_cols, src_rows = partial_terms.shape
    run_len = rcv_cols // src_count
    runs_view = partial_terms.reshape(freq_count, chan_count, src_count, run_len, src_rows)
    padded = extended(runs_view.astype(jnp.bfloat16), (("rcv", 3),), REACH, True).astype(
        runs_view.dtype
    )
    lower_rim = padded[:, :, :, :REACH]
    middle = padded[:, :, :, REACH : REACH + run_len]
    upper_rim = padded[:, :, :, REACH + run_len :]
    zero_rim = jnp.zeros_like(lower_rim[:, :, :1])
    lower_rim = jnp.where(
        rcv_pos == 0, jnp.concatenate([zero_rim, lower_rim[:, :, :-1]], axis=2), lower_rim
    )
    upper_rim = jnp.where(
        rcv_pos == rcv_count - 1,
        jnp.concatenate([upper_rim[:, :, 1:], zero_rim], axis=2),
        upper_rim,
    )
    padded = jnp.concatenate([lower_rim, middle, upper_rim], axis=3)
    recv_total = padded[:, :, :, 0:run_len]
    for shift_pos in range(1, 2 * REACH + 1):
        recv_total = recv_total + padded[:, :, :, shift_pos : shift_pos + run_len]
    recv_total = recv_total.reshape(freq_count, chan_count, rcv_cols, src_rows)
    src_padded = extended(recv_total.astype(jnp.bfloat16), (("src", 3),), REACH, False).astype(
        recv_total.dtype
    )
    box_totals = src_padded[..., 0:src_rows]
    for shift_pos in range(1, 2 * REACH + 1):
        box_totals = box_totals + src_padded[..., shift_pos : shift_pos + src_rows]
    return box_totals


def run_sweeps(data_bf, pred_bf, summer):
    data_f32 = data_bf.astype(jnp.float32)
    pred_f32 = pred_bf.astype(jnp.float32)
    data_real = data_f32[:, 0]
    data_imag = data_f32[:, 1]
    pred_real = pred_f32[:, 0]
    pred_imag = pred_f32[:, 1]
    err_real = data_real
    err_imag = data_imag
    for sweep_step in range(SWEEPS):
        weight = 1.5 - jnp.tanh(err_real * err_real + err_imag * err_imag)
        partial_terms = jnp.stack(
            [
                weight * (pred_real * data_real + pred_imag * data_imag),
                weight * (pred_real * data_imag - pred_imag * data_real),
                weight * (pred_real * pred_real + pred_imag * pred_imag),
            ],
            axis=1,
        )
        box_totals = summer(partial_terms)
        denom = box_totals[:, 2] + weight_eps
        gain_real = box_totals[:, 0] / denom
        gain_imag = box_totals[:, 1] / denom
        err_real = data_real - (gain_real * pred_real - gain_imag * pred_imag)
        err_imag = data_imag - (gain_real * pred_imag + gain_imag * pred_real)
    return jnp.stack([err_real, err_imag], axis=1)


def plain_shards(record, panel_offset):
    src_count = lax.axis_size("src")
    rcv_count = lax.axis_size("rcv")
    src_pos = lax.axis_index("src")
    rcv_pos = lax.axis_index("rcv")
    rcv_cols = record.shape[2]
    src_rows = record.shape[3]
    run_len = rcv_cols // src_count
    per_run = run_len // STRIDE
    panel_len = panel_offset.shape[0]
    run_ids = jnp.arange(src_count, dtype=jnp.int32)[:, None]
    within = jnp.arange(per_run, dtype=jnp.int32)[None, :]
    col_groups = (src_rows * run_ids + run_len * rcv_pos) // STRIDE + within
    col_index = (run_len * run_ids + STRIDE * within + jnp.take(panel_offset, col_groups)).reshape(
        -1
    )
    row_groups = jnp.arange(src_rows // STRIDE, dtype=jnp.int32)
    row_index = STRIDE * row_groups + jnp.take(
        panel_offset, src_rows // STRIDE * src_pos + row_groups
    )
    col_piece = jnp.swapaxes(jnp.take(record, col_index, axis=2), 2, 3)
    row_piece = jnp.take(record, row_index, axis=3)
    own_front = reorder_keys(
        lax.all_to_all(col_piece, "rcv", split_axis=2, concat_axis=3, tiled=True),
        rcv_count,
        src_count,
    )
    own_behind = lax.all_to_all(row_piece, "src", split_axis=2, concat_axis=3, tiled=True)
    owned_rows = average_pair(own_front, own_behind)
    right_side = lax.all_gather(owned_rows, "src", axis=2, tiled=True)
    prediction = predict_block(right_side, lax.all_gather(owned_rows, "rcv", axis=2, tiled=True))
    pred_round = lax.optimization_barrier(prediction.astype(jnp.bfloat16))
    multiples = (prediction * panel_len ** (-0.5)).astype(jnp.bfloat16)

    def runs_total(partial_terms):
        return neighbour_sum(partial_terms, src_count, rcv_pos, rcv_count)

    primaries = run_sweeps(record, pred_round, runs_total).astype(jnp.bfloat16)
    return (primaries, multiples)

HALO = 2 * REACH
MESH = pl.DeviceIdType.MESH


def wide_spans(width):
    spans = [(start, 256) for start in range(0, width - 255, 256)]
    done = 256 * (width // 256)
    return spans + ([(done, width - done)] if done < width else [])


def band(shape, shift, period):
    rows = lax.broadcasted_iota(jnp.int32, shape, 0)
    cols = lax.broadcasted_iota(jnp.int32, shape, 1) + shift
    gap = jnp.abs(rows - cols)
    if period:
        gap = jnp.minimum(gap, period - gap)
    return jnp.where(gap <= REACH, 1.0, 0.0).astype(jnp.bfloat16)


def sweep_kernel(
    scale, record_ref, rim_ref, side_ref, right_ref, left_ref, prim_ref, mult_ref,
    left_all, right_all, data, pred32, predb, terms, partial, totals, row_band, lane_band
):
    runs_len = record_ref.shape[2]
    src_rows = record_ref.shape[3]
    owners = left_ref.shape[0]
    rows = runs_len + 2 * HALO
    width = src_rows + 128
    panel = left_ref.shape[3]
    f32, bf = jnp.float32, jnp.bfloat16

    @pl.when(pl.program_id(0) == 0)
    def _():
        row_band[...] = band((rows, rows), 0, rows)
        lane_band[...] = band((512, 256), 128, 0)
        left_all[src_rows:, :] = jnp.zeros((128, 2 * panel), bf)
        for chan in range(2):
            lanes = slice(chan * panel, (chan + 1) * panel)
            for owner in range(owners):
                left_all[owner * runs_len : (owner + 1) * runs_len, lanes] = left_ref[
                    owner, chan, :runs_len
                ]
            after = left_ref[owners - 1, chan, runs_len:]
            before = left_ref[0, chan, runs_len:]
            spot = lax.broadcasted_iota(jnp.int32, after.shape, 0)
            zero = jnp.zeros_like(after)
            left_all[src_rows : src_rows + 2 * HALO, lanes] = jnp.where(spot < HALO, after, zero)
            left_all[width - 2 * HALO : width, lanes] = jnp.where(spot >= HALO, before, zero)

    for chan in range(2):
        data[chan, :runs_len, :src_rows] = record_ref[0, chan]
        data[chan, runs_len:, :src_rows] = rim_ref[chan, 0]
        data[chan, :, src_rows:] = side_ref[chan, 0]
    right_real = right_ref[0, 0]
    right_imag = right_ref[0, 1]
    right_all[:rows, :panel] = right_real
    right_all[:rows, panel:] = -right_imag
    right_all[rows:, :panel] = right_imag
    right_all[rows:, panel:] = right_real
    for start, size in wide_spans(width):
        pred32[:, start : start + size] = lax.dot_general(
            right_all[...],
            left_all[start : start + size, :],
            (((1,), (1,)), ((), ())),
            preferred_element_type=f32,
        )

    def put_terms(at, lanes, err, here, guess):
        weight = 1.5 - jnp.tanh(err[0] * err[0] + err[1] * err[1])
        parts = (
            guess[0] * here[0] + guess[1] * here[1],
            guess[0] * here[1] - guess[1] * here[0],
            guess[0] * guess[0] + guess[1] * guess[1],
        )
        for index, part in enumerate(parts):
            terms[index, at, lanes] = (weight * part).astype(bf)

    def new_err(at, lanes):
        here = [data[chan, at, lanes].astype(f32) for chan in range(2)]
        guess = [predb[chan, at, lanes].astype(f32) for chan in range(2)]
        inverse = 1.0 / (totals[2, at, lanes] + weight_eps)
        gain_real = totals[0, at, lanes] * inverse
        gain_imag = totals[1, at, lanes] * inverse
        err = (
            here[0] - (gain_real * guess[0] - gain_imag * guess[1]),
            here[1] - (gain_real * guess[1] + gain_imag * guess[0]),
        )
        return err, here, guess

    def box():
        for index in range(3):
            for start, size in wide_spans(width):
                partial[index, :, 128 + start : 128 + start + size] = jnp.dot(
                    row_band[...], terms[index, :, start : start + size], preferred_element_type=f32
                ).astype(bf)
            partial[index, :, :128] = partial[index, :, width : width + 128]
            partial[index, :, width + 128 :] = partial[index, :, 128:256]
        for index in range(3):
            for start, size in wide_spans(width):
                totals[index, :, start : start + size] = jnp.dot(
                    partial[index, :, start : start + size + 256],
                    lane_band[: size + 256, :size],
                    preferred_element_type=f32,
                )

    @pl.loop(0, rows // 16)
    def _(step):
        at = pl.ds(pl.multiple_of(step * 16, 16), 16)
        at_imag = pl.ds(pl.multiple_of(rows + step * 16, 16), 16)
        for block in range(width // 128):
            lanes = slice(block * 128, (block + 1) * 128)
            here = [data[chan, at, lanes].astype(f32) for chan in range(2)]
            guess = []
            for chan, spot in enumerate((at, at_imag)):
                rounded = pred32[spot, lanes].astype(bf)
                predb[chan, at, lanes] = rounded
                guess.append(rounded.astype(f32))
            put_terms(at, lanes, here, here, guess)

    @pl.loop(0, runs_len // 16)
    def _(step):
        at = pl.ds(pl.multiple_of(step * 16, 16), 16)
        at_imag = pl.ds(pl.multiple_of(rows + step * 16, 16), 16)
        for block in range(src_rows // 128):
            lanes = slice(block * 128, (block + 1) * 128)
            mult_ref[0, 0, at, lanes] = (pred32[at, lanes] * scale).astype(bf)
            mult_ref[0, 1, at, lanes] = (pred32[at_imag, lanes] * scale).astype(bf)

    for sweep_step in range(SWEEPS - 1):
        box()

        @pl.loop(0, rows // 16)
        def _(step):
            at = pl.ds(pl.multiple_of(step * 16, 16), 16)
            for block in range(width // 128):
                lanes = slice(block * 128, (block + 1) * 128)
                put_terms(at, lanes, *new_err(at, lanes))

    box()

    @pl.loop(0, runs_len // 16)
    def _(step):
        at = pl.ds(pl.multiple_of(step * 16, 16), 16)
        for block in range(src_rows // 128):
            lanes = slice(block * 128, (block + 1) * 128)
            err, _, _ = new_err(at, lanes)
            prim_ref[0, 0, at, lanes] = err[0].astype(bf)
            prim_ref[0, 1, at, lanes] = err[1].astype(bf)


def sweep_call(record, rims, sides, right, left):
    _, _, rcv_cols, src_rows = record.shape
    runs = right.shape[0]
    run_len = rcv_cols // runs
    rows = run_len + 2 * HALO
    width = src_rows + 128
    panel = left.shape[3]
    f32, bf = jnp.float32, jnp.bfloat16
    out = jax.ShapeDtypeStruct(record.shape, bf)
    tile = pl.BlockSpec((1, 2, run_len, src_rows), lambda r: (0, 0, r, 0))
    return pl.pallas_call(
        functools.partial(sweep_kernel, panel ** (-0.5)),
        grid=(runs,),
        out_shape=(out, out),
        in_specs=[
            tile,
            pl.BlockSpec((2, 1, 2 * HALO, src_rows), lambda r: (0, r, 0, 0)),
            pl.BlockSpec((2, 1, rows, 128), lambda r: (0, r, 0, 0)),
            pl.BlockSpec((1, 2, rows, panel), lambda r: (r, 0, 0, 0)),
            pl.BlockSpec(left.shape, lambda r: (0, 0, 0, 0), pipeline_mode=pl.Buffered(1)),
        ],
        out_specs=(tile, tile),
        scratch_shapes=[
            pltpu.VMEM((width, 2 * panel), bf),
            pltpu.VMEM((2 * rows, 2 * panel), bf),
            pltpu.VMEM((2, rows, width), bf),
            pltpu.VMEM((2 * rows, width), f32),
            pltpu.VMEM((2, rows, width), bf),
            pltpu.VMEM((3, rows, width), bf),
            pltpu.VMEM((3, rows, width + 256), bf),
            pltpu.VMEM((3, rows, width), f32),
            pltpu.VMEM((rows, rows), bf),
            pltpu.VMEM((512, 256), bf),
        ],
        compiler_params=pltpu.CompilerParams(vmem_limit_bytes=56 * 1024 * 1024),
        cost_estimate=pl.CostEstimate(
            flops=20_000_000_000, bytes_accessed=4 * record.size * 2, transcendentals=2 * record.size
        ),
    )(record, rims, sides, right, left)


def panel_places(panel_offset, src_count, rcv_count, src_pos, rcv_pos, run_len, src_rows):
    per_run = run_len // STRIDE
    run_ids = jnp.arange(src_count, dtype=jnp.int32)[:, None]
    within = jnp.arange(per_run, dtype=jnp.int32)[None, :]
    by_block = panel_offset.reshape(src_count, rcv_count, per_run)
    mine = lax.dynamic_index_in_dim(by_block, rcv_pos, axis=1, keepdims=False)
    col_index = (run_len * run_ids + STRIDE * within + mine).reshape(-1)
    groups = jnp.arange(src_rows // STRIDE, dtype=jnp.int32)
    row_index = STRIDE * groups + lax.dynamic_index_in_dim(
        panel_offset.reshape(src_count, -1), src_pos, axis=0, keepdims=False
    )
    return col_index, row_index

def exchange_kernel(
    sizes, rec, col_pick, row_pick, left, right, rims, sides,
    front_tx, front_rx, behind_tx, behind_rx, head_tx, head_rx, tail_tx, tail_rx,
    first_tx, after_rx, last_tx, before_rx, own, next_rx, prev_rx,
    front_send, front_recv, behind_send, behind_recv, edge_send, edge_recv,
    right_send, right_recv, line_send, left_recv, pair_send,
):
    srcs, rcvs = sizes
    src = lax.axis_index("src")
    rcv = lax.axis_index("rcv")
    f32, bf = jnp.float32, jnp.bfloat16
    rcv_cols, src_rows = rec.shape[1:]
    run_len = rcv_cols // srcs
    rows = run_len + 2 * HALO
    panel = left.shape[3]
    each = panel // (srcs * rcvs)
    spots = rcvs // 2
    spot, core = rcv // 2, lax.rem(rcv, 2)

    def remote(source, target, send, recv, where):
        return pltpu.make_async_remote_copy(
            src_ref=source, dst_ref=target, send_sem=send, recv_sem=recv,
            device_id=where, device_id_type=MESH,
        )

    rcv_peers = [lax.rem(rcv + step, rcvs) for step in range(1, rcvs)]
    src_peers = [lax.rem(src + step, srcs) for step in range(1, srcs)]
    last_rcv, first_rcv = rcv == rcvs - 1, rcv == 0
    has_next = jnp.logical_not(jnp.logical_and(last_rcv, src == srcs - 1))
    has_prev = jnp.logical_not(jnp.logical_and(first_rcv, src == 0))
    next_dev = (
        jnp.where(last_rcv, jnp.minimum(src + 1, srcs - 1), src), jnp.where(last_rcv, 0, rcv + 1)
    )
    prev_dev = (
        jnp.where(first_rcv, jnp.maximum(src - 1, 0), src), jnp.where(first_rcv, rcvs - 1, rcv - 1)
    )
    far_next = jnp.logical_and(last_rcv, src < srcs - 1)
    far_prev = jnp.logical_and(first_rcv, src > 0)

    barrier = pltpu.get_barrier_semaphore()
    for peer in rcv_peers:
        pl.semaphore_signal(barrier, inc=1, device_id=(src, peer), device_id_type=MESH)
    for peer in src_peers:
        pl.semaphore_signal(barrier, inc=1, device_id=(peer, rcv), device_id_type=MESH)

    @pl.when(far_next)
    def _():
        pl.semaphore_signal(barrier, inc=1, device_id=next_dev, device_id_type=MESH)

    @pl.when(far_prev)
    def _():
        pl.semaphore_signal(barrier, inc=1, device_id=prev_dev, device_id_type=MESH)

    for chan in range(2):
        for pair in range(srcs // 2):
            for buffer, start in ((head_tx, 0), (tail_tx, run_len - 16)):
                tiles = [
                    rec[chan, run * run_len + start : run * run_len + start + 16].astype(f32)
                    for run in (2 * pair, 2 * pair + 1)
                ]
                part = slice(0, HALO) if start == 0 else slice(16 - HALO, 16)
                buffer[chan, 16 * pair : 16 * pair + 16] = jnp.concatenate(
                    [tile[part] for tile in tiles], axis=0
                ).astype(bf)
        picked = lax.dot_general(
            rec[chan], col_pick[...], (((0,), (0,)), ((), ())), preferred_element_type=f32
        ).astype(bf)
        for peer in range(rcvs):
            front_tx[peer, chan] = picked[peer * run_len : (peer + 1) * run_len]

    pl.semaphore_wait(
        barrier,
        rcvs - 1 + srcs - 1 + jnp.where(far_next, 1, 0) + jnp.where(far_prev, 1, 0),
    )

    fronts = []
    for index, peer in enumerate(rcv_peers):
        copy = remote(
            front_tx.at[peer], front_rx.at[rcv], front_send.at[index], front_recv.at[rcv], (src, peer)
        )
        copy.start()
        fronts.append(copy)
    front_rx[rcv] = front_tx[rcv]
    heads = remote(
        head_tx, head_rx, edge_send.at[0], edge_recv.at[0], (src, lax.rem(rcv + rcvs - 1, rcvs))
    )
    tails = remote(tail_tx, tail_rx, edge_send.at[1], edge_recv.at[1], (src, lax.rem(rcv + 1, rcvs)))
    heads.start()
    tails.start()

    for chan in range(2):
        picked = jnp.dot(rec[chan], row_pick[...], preferred_element_type=f32).astype(bf)
        for peer in range(srcs):
            behind_tx[peer, chan] = picked[peer * run_len : (peer + 1) * run_len]
    behinds = []
    for index, peer in enumerate(src_peers):
        copy = remote(
            behind_tx.at[peer], behind_rx.at[src], behind_send.at[index], behind_recv.at[src],
            (peer, rcv),
        )
        copy.start()
        behinds.append(copy)
    behind_rx[src] = behind_tx[src]

    heads.wait()
    tails.wait()

    def edge(buffer, chan, run):
        if run < 0 or run >= srcs:
            return jnp.zeros((HALO, src_rows), f32)
        tile = buffer[chan, run // 2 * 16 : run // 2 * 16 + 16].astype(f32)
        return tile[run % 2 * HALO : run % 2 * HALO + HALO]

    for chan in range(2):
        for run in range(srcs):
            below = jnp.where(last_rcv, edge(head_rx, chan, run + 1), edge(head_rx, chan, run))
            above = jnp.where(first_rcv, edge(tail_rx, chan, run - 1), edge(tail_rx, chan, run))
            rim = jnp.concatenate([below, above], axis=0).astype(bf)
            rims[chan, run] = rim
            main = slice(run * run_len, (run + 1) * run_len)
            first_tx[chan, run, :run_len] = rec[chan, main, :128]
            first_tx[chan, run, run_len:] = rim[:, :128]
            last_tx[chan, run, :run_len] = rec[chan, main, src_rows - 128 :]
            last_tx[chan, run, run_len:] = rim[:, src_rows - 128 :]

    low = jnp.maximum(src - 1, 0)
    high = jnp.minimum(src + 1, srcs - 1)
    firsts = remote(first_tx, after_rx, edge_send.at[2], edge_recv.at[2], (low, rcv))
    lasts = remote(last_tx, before_rx, edge_send.at[3], edge_recv.at[3], (high, rcv))

    @pl.when(src > 0)
    def _():
        firsts.start()

    @pl.when(src < srcs - 1)
    def _():
        lasts.start()

    for index, step in enumerate(range(1, rcvs)):
        peer = lax.rem(rcv + rcvs - step, rcvs)
        remote(
            front_tx.at[peer], front_rx.at[peer], front_send.at[index], front_recv.at[peer],
            (src, peer),
        ).wait_recv()
    for index, step in enumerate(range(1, srcs)):
        peer = lax.rem(src + srcs - step, srcs)
        remote(
            behind_tx.at[peer], behind_rx.at[peer], behind_send.at[index], behind_recv.at[peer],
            (peer, rcv),
        ).wait_recv()

    for chan in range(2):
        total = jnp.zeros((run_len, panel), f32)
        for peer in range(rcvs):
            shape = (srcs * each, panel)
            index = lax.broadcasted_iota(jnp.int32, shape, 0)
            column = lax.broadcasted_iota(jnp.int32, shape, 1)
            aim = index // each * (rcvs * each) + peer * each + index % each
            pick = jnp.where(column == aim, 1.0, 0.0).astype(bf)
            total = total + jnp.dot(front_rx[peer, chan], pick, preferred_element_type=f32)
        for peer in range(srcs):
            shape = (rcvs * each, panel)
            index = lax.broadcasted_iota(jnp.int32, shape, 0)
            column = lax.broadcasted_iota(jnp.int32, shape, 1)
            pick = jnp.where(column == index + peer * rcvs * each, 1.0, 0.0).astype(bf)
            total = total + jnp.dot(behind_rx[peer, chan], pick, preferred_element_type=f32)
        own[chan, :run_len] = (total * 0.5).astype(bf)

    to_prev = remote(own.at[:, pl.ds(0, 16)], next_rx, edge_send.at[4], edge_recv.at[4], prev_dev)
    to_next = remote(
        own.at[:, pl.ds(run_len - 16, 16)], prev_rx, edge_send.at[5], edge_recv.at[5], next_dev
    )

    @pl.when(has_prev)
    def _():
        to_prev.start()

    @pl.when(has_next)
    def _():
        to_next.start()

    @pl.when(has_next)
    def _():
        to_prev.wait_recv()

    @pl.when(jnp.logical_not(has_next))
    def _():
        next_rx[...] = jnp.zeros_like(next_rx)

    @pl.when(has_prev)
    def _():
        to_next.wait_recv()

    @pl.when(jnp.logical_not(has_prev))
    def _():
        prev_rx[...] = jnp.zeros_like(prev_rx)

    place = lax.broadcasted_iota(jnp.int32, (2, 2 * HALO, panel), 1)
    own[:, run_len:] = jnp.where(place < HALO, next_rx[...], prev_rx[...])

    def line(owner_spot, source, up, step):
        owner = 2 * owner_spot + core
        shift = 2 if up else -2
        return remote(
            source, left.at[owner], line_send.at[0 if up else 1, step], left_recv.at[owner],
            (src, jnp.clip(rcv + shift, 0, rcvs - 1)),
        )

    def hand(owner, source):
        return remote(
            source, left.at[owner], pair_send.at[owner // 2], left_recv.at[owner],
            (src, rcv + 1 - 2 * core),
        )

    @pl.when(spot < spots - 1)
    def _():
        line(spot, own, True, 0).start()

    @pl.when(spot > 0)
    def _():
        line(spot, own, False, 0).start()

    rights = []
    for index, peer in enumerate(src_peers):
        copy = remote(own, right.at[src], right_send.at[index], right_recv.at[src], (peer, rcv))
        copy.start()
        rights.append(copy)
    hand(rcv, own).start()
    left[rcv] = own[...]
    right[src] = own[...]

    for step in range(1, spots):
        for up in (True, False):
            owner_spot = spot - step if up else spot + step
            arrives = spot >= step if up else spot + step < spots
            onward = spot < spots - 1 if up else spot > 0

            @pl.when(arrives)
            def _():
                owner = 2 * owner_spot + core
                line(owner_spot, left.at[owner], up, step - 1).wait_recv()
                if step < spots - 1:

                    @pl.when(onward)
                    def _():
                        line(owner_spot, left.at[owner], up, step).start()

                hand(owner, left.at[owner]).start()

    for copy in fronts + behinds:
        copy.wait_send()

    @pl.when(src > 0)
    def _():
        firsts.wait_send()
        lasts.wait_recv()

    @pl.when(src < srcs - 1)
    def _():
        lasts.wait_send()
        firsts.wait_recv()

    @pl.when(src == 0)
    def _():
        before_rx[...] = jnp.zeros_like(before_rx)

    @pl.when(src == srcs - 1)
    def _():
        after_rx[...] = jnp.zeros_like(after_rx)

    lane = lax.broadcasted_iota(jnp.int32, (rows, 128), 1)
    zero = jnp.zeros((rows, 128), bf)
    for chan in range(2):
        for run in range(srcs):
            sides[chan, run] = jnp.where(
                lane < HALO, after_rx[chan, run], jnp.where(lane >= 128 - HALO, before_rx[chan, run], zero)
            )

    @pl.when(has_prev)
    def _():
        to_prev.wait_send()

    @pl.when(has_next)
    def _():
        to_next.wait_send()

    for copy in rights:
        copy.wait_send()
    for step in range(1, srcs):
        peer = lax.rem(src + srcs - step, srcs)
        remote(own, right.at[peer], right_send.at[0], right_recv.at[peer], (peer, rcv)).wait_recv()
    for step in range(spots - 1):
        @pl.when(jnp.logical_and(spot < spots - 1, spot >= step))
        def _():
            line(spot, own, True, step).wait_send()

        @pl.when(jnp.logical_and(spot > 0, spot + step < spots))
        def _():
            line(spot, own, False, step).wait_send()

    for index in range(spots):
        hand(2 * index + core, own).wait_send()
        hand(2 * index + 1 - core, own).wait_recv()


def exchange_call(rec, col_pick, row_pick, srcs, rcvs, panel):
    _, rcv_cols, src_rows = rec.shape
    run_len = rcv_cols // srcs
    rows = run_len + 2 * HALO
    bf = jnp.bfloat16
    vmem = pl.BlockSpec(memory_space=pltpu.VMEM)
    front = (rcvs, 2, run_len, col_pick.shape[1])
    behind = (srcs, 2, run_len, row_pick.shape[1])
    edges = (2, HALO * srcs, src_rows)
    side = (2, srcs, rows, 128)
    shapes = [front, front, behind, behind, edges, edges, edges, edges, side, side, side, side]
    shapes += [(2, rows, panel), (2, 16, panel), (2, 16, panel)]
    dma = pltpu.SemaphoreType.DMA
    return pl.pallas_call(
        functools.partial(exchange_kernel, (srcs, rcvs)),
        out_shape=(
            jax.ShapeDtypeStruct((rcvs, 2, rows, panel), bf),
            jax.ShapeDtypeStruct((srcs, 2, rows, panel), bf),
            jax.ShapeDtypeStruct((2, srcs, 2 * HALO, src_rows), bf),
            jax.ShapeDtypeStruct(side, bf),
        ),
        in_specs=[vmem] * 3,
        out_specs=(vmem,) * 4,
        scratch_shapes=[pltpu.VMEM(shape, bf) for shape in shapes]
        + [
            dma((rcvs,)), dma((rcvs,)), dma((srcs,)), dma((srcs,)), dma((6,)), dma((6,)),
            dma((srcs,)), dma((srcs,)), dma((2, rcvs // 2)), dma((rcvs,)), dma((rcvs // 2,)),
        ],
        compiler_params=pltpu.CompilerParams(
            collective_id=0, has_side_effects=True, vmem_limit_bytes=48 * 1024 * 1024
        ),
        cost_estimate=pl.CostEstimate(
            flops=2_000_000_000, bytes_accessed=8 * rec.size, transcendentals=0
        ),
    )(rec, col_pick, row_pick)


def shards(record, panel_offset):
    src_count = lax.axis_size("src")
    rcv_count = lax.axis_size("rcv")
    freqs, _, rcv_cols, src_rows = record.shape
    run_len = rcv_cols // src_count
    if freqs != 1 or run_len % 16 or src_rows % 128 or src_count % 2 or rcv_count % 2:
        return plain_shards(record, panel_offset)
    src_pos = lax.axis_index("src")
    rcv_pos = lax.axis_index("rcv")
    panel = panel_offset.shape[0]
    col_index, row_index = panel_places(
        panel_offset, src_count, rcv_count, src_pos, rcv_pos, run_len, src_rows
    )
    rec = record[0]
    col_pick = (jnp.arange(rcv_cols)[:, None] == col_index[None, :]).astype(record.dtype)
    row_pick = (jnp.arange(src_rows)[:, None] == row_index[None, :]).astype(record.dtype)
    left, right, rims, sides = exchange_call(rec, col_pick, row_pick, src_count, rcv_count, panel)
    return sweep_call(record, rims, sides, right, left)


def solution(mesh):
    in_specs = (P(None, None, "rcv", "src"), P())
    out_specs = (P(None, None, "rcv", "src"), P(None, None, "rcv", "src"))
    return jax.shard_map(shards, mesh=mesh, in_specs=in_specs, out_specs=out_specs, check_vma=False)
```

```python
import functools

import jax
import jax.numpy as jnp
from jax import lax
from jax.experimental import pallas as pl
from jax.experimental.pallas import tpu as pltpu
from jax.sharding import PartitionSpec as P

STRIDE = 8
REACH = 4
SWEEPS = 2


weight_eps = 1e-06


def extended(cells, sides, width, closed):
    for axis, dim in sides:
        count = lax.axis_size(axis)
        ends = count if closed else count - 1
        head = lax.slice_in_dim(cells, 0, width, axis=dim)
        tail = lax.slice_in_dim(cells, cells.shape[dim] - width, cells.shape[dim], axis=dim)
        cells = jnp.concatenate(
            [
                lax.ppermute(tail, axis, [(i, (i + 1) % count) for i in range(ends)]),
                cells,
                lax.ppermute(head, axis, [((i + 1) % count, i) for i in range(ends)]),
            ],
            axis=dim,
        )
    return cells


def reorder_keys(values, rcv_count, src_count):
    full_shape = values.shape
    grouped = values.reshape(
        full_shape[:-1] + (rcv_count, src_count, full_shape[-1] // (rcv_count * src_count))
    )
    return jnp.swapaxes(grouped, -3, -2).reshape(full_shape)


def average_pair(first_part, second_part):
    return ((first_part.astype(jnp.float32) + second_part.astype(jnp.float32)) * 0.5).astype(
        jnp.bfloat16
    )


def cross_dot(left_mat, right_mat):
    return lax.dot_general(
        left_mat, right_mat, (((2,), (2,)), ((0,), (0,))), preferred_element_type=jnp.float32
    )


def predict_block(right_side, left_side):
    right_real = right_side[:, 0]
    right_imag = right_side[:, 1]
    left_real = left_side[:, 0]
    left_imag = left_side[:, 1]
    pred_real = cross_dot(right_real, left_real) - cross_dot(right_imag, left_imag)
    pred_imag = cross_dot(right_real, left_imag) + cross_dot(right_imag, left_real)
    return jnp.stack([pred_real, pred_imag], axis=1)


def neighbour_sum(partial_terms, src_count, rcv_pos, rcv_count):
    freq_count, chan_count, rcv_cols, src_rows = partial_terms.shape
    run_len = rcv_cols // src_count
    runs_view = partial_terms.reshape(freq_count, chan_count, src_count, run_len, src_rows)
    padded = extended(runs_view.astype(jnp.bfloat16), (("rcv", 3),), REACH, True).astype(
        runs_view.dtype
    )
    lower_rim = padded[:, :, :, :REACH]
    middle = padded[:, :, :, REACH : REACH + run_len]
    upper_rim = padded[:, :, :, REACH + run_len :]
    zero_rim = jnp.zeros_like(lower_rim[:, :, :1])
    lower_rim = jnp.where(
        rcv_pos == 0, jnp.concatenate([zero_rim, lower_rim[:, :, :-1]], axis=2), lower_rim
    )
    upper_rim = jnp.where(
        rcv_pos == rcv_count - 1,
        jnp.concatenate([upper_rim[:, :, 1:], zero_rim], axis=2),
        upper_rim,
    )
    padded = jnp.concatenate([lower_rim, middle, upper_rim], axis=3)
    recv_total = padded[:, :, :, 0:run_len]
    for shift_pos in range(1, 2 * REACH + 1):
        recv_total = recv_total + padded[:, :, :, shift_pos : shift_pos + run_len]
    recv_total = recv_total.reshape(freq_count, chan_count, rcv_cols, src_rows)
    src_padded = extended(recv_total.astype(jnp.bfloat16), (("src", 3),), REACH, False).astype(
        recv_total.dtype
    )
    box_totals = src_padded[..., 0:src_rows]
    for shift_pos in range(1, 2 * REACH + 1):
        box_totals = box_totals + src_padded[..., shift_pos : shift_pos + src_rows]
    return box_totals


def run_sweeps(data_bf, pred_bf, summer):
    data_f32 = data_bf.astype(jnp.float32)
    pred_f32 = pred_bf.astype(jnp.float32)
    data_real = data_f32[:, 0]
    data_imag = data_f32[:, 1]
    pred_real = pred_f32[:, 0]
    pred_imag = pred_f32[:, 1]
    err_real = data_real
    err_imag = data_imag
    for sweep_step in range(SWEEPS):
        weight = 1.5 - jnp.tanh(err_real * err_real + err_imag * err_imag)
        partial_terms = jnp.stack(
            [
                weight * (pred_real * data_real + pred_imag * data_imag),
                weight * (pred_real * data_imag - pred_imag * data_real),
                weight * (pred_real * pred_real + pred_imag * pred_imag),
            ],
            axis=1,
        )
        box_totals = summer(partial_terms)
        denom = box_totals[:, 2] + weight_eps
        gain_real = box_totals[:, 0] / denom
        gain_imag = box_totals[:, 1] / denom
        err_real = data_real - (gain_real * pred_real - gain_imag * pred_imag)
        err_imag = data_imag - (gain_real * pred_imag + gain_imag * pred_real)
    return jnp.stack([err_real, err_imag], axis=1)


def plain_shards(record, panel_offset):
    src_count = lax.axis_size("src")
    rcv_count = lax.axis_size("rcv")
    src_pos = lax.axis_index("src")
    rcv_pos = lax.axis_index("rcv")
    rcv_cols = record.shape[2]
    src_rows = record.shape[3]
    run_len = rcv_cols // src_count
    per_run = run_len // STRIDE
    panel_len = panel_offset.shape[0]
    run_ids = jnp.arange(src_count, dtype=jnp.int32)[:, None]
    within = jnp.arange(per_run, dtype=jnp.int32)[None, :]
    col_groups = (src_rows * run_ids + run_len * rcv_pos) // STRIDE + within
    col_index = (run_len * run_ids + STRIDE * within + jnp.take(panel_offset, col_groups)).reshape(
        -1
    )
    row_groups = jnp.arange(src_rows // STRIDE, dtype=jnp.int32)
    row_index = STRIDE * row_groups + jnp.take(
        panel_offset, src_rows // STRIDE * src_pos + row_groups
    )
    col_piece = jnp.swapaxes(jnp.take(record, col_index, axis=2), 2, 3)
    row_piece = jnp.take(record, row_index, axis=3)
    own_front = reorder_keys(
        lax.all_to_all(col_piece, "rcv", split_axis=2, concat_axis=3, tiled=True),
        rcv_count,
        src_count,
    )
    own_behind = lax.all_to_all(row_piece, "src", split_axis=2, concat_axis=3, tiled=True)
    owned_rows = average_pair(own_front, own_behind)
    right_side = lax.all_gather(owned_rows, "src", axis=2, tiled=True)
    prediction = predict_block(right_side, lax.all_gather(owned_rows, "rcv", axis=2, tiled=True))
    pred_round = lax.optimization_barrier(prediction.astype(jnp.bfloat16))
    multiples = (prediction * panel_len ** (-0.5)).astype(jnp.bfloat16)

    def runs_total(partial_terms):
        return neighbour_sum(partial_terms, src_count, rcv_pos, rcv_count)

    primaries = run_sweeps(record, pred_round, runs_total).astype(jnp.bfloat16)
    return (primaries, multiples)

HALO = 2 * REACH
MESH = pl.DeviceIdType.MESH


def wide_spans(width):
    spans = [(start, 256) for start in range(0, width - 255, 256)]
    done = 256 * (width // 256)
    return spans + ([(done, width - done)] if done < width else [])


def band(shape, shift, period):
    rows = lax.broadcasted_iota(jnp.int32, shape, 0)
    cols = lax.broadcasted_iota(jnp.int32, shape, 1) + shift
    gap = jnp.abs(rows - cols)
    if period:
        gap = jnp.minimum(gap, period - gap)
    return jnp.where(gap <= REACH, 1.0, 0.0).astype(jnp.bfloat16)


def sweep_kernel(
    scale, record_ref, rim_ref, side_ref, pred_ref, prim_ref, mult_ref,
    data, predb, terms, partial, totals, row_band, lane_band
):
    runs_len = record_ref.shape[2]
    src_rows = record_ref.shape[3]
    rows = runs_len + 2 * HALO
    width = src_rows + 128
    f32, bf = jnp.float32, jnp.bfloat16

    @pl.when(pl.program_id(0) == 0)
    def _():
        row_band[...] = band((rows, rows), 0, rows)
        lane_band[...] = band((512, 256), 128, 0)

    for chan in range(2):
        data[chan, :runs_len, :src_rows] = record_ref[0, chan]
        data[chan, runs_len:, :src_rows] = rim_ref[chan, 0]
        data[chan, :, src_rows:] = side_ref[chan, 0]

    def put_terms(at, lanes, err, here, guess):
        weight = 1.5 - jnp.tanh(err[0] * err[0] + err[1] * err[1])
        parts = (
            guess[0] * here[0] + guess[1] * here[1],
            guess[0] * here[1] - guess[1] * here[0],
            guess[0] * guess[0] + guess[1] * guess[1],
        )
        for index, part in enumerate(parts):
            terms[index, at, lanes] = (weight * part).astype(bf)

    def new_err(at, lanes):
        here = [data[chan, at, lanes].astype(f32) for chan in range(2)]
        guess = [predb[chan, at, lanes].astype(f32) for chan in range(2)]
        inverse = 1.0 / (totals[2, at, lanes] + weight_eps)
        gain_real = totals[0, at, lanes] * inverse
        gain_imag = totals[1, at, lanes] * inverse
        err = (
            here[0] - (gain_real * guess[0] - gain_imag * guess[1]),
            here[1] - (gain_real * guess[1] + gain_imag * guess[0]),
        )
        return err, here, guess

    def box():
        for index in range(3):
            for start, size in wide_spans(width):
                partial[index, :, 128 + start : 128 + start + size] = jnp.dot(
                    row_band[...], terms[index, :, start : start + size], preferred_element_type=f32
                ).astype(bf)
            partial[index, :, :128] = partial[index, :, width : width + 128]
            partial[index, :, width + 128 :] = partial[index, :, 128:256]
        for index in range(3):
            for start, size in wide_spans(width):
                totals[index, :, start : start + size] = jnp.dot(
                    partial[index, :, start : start + size + 256],
                    lane_band[: size + 256, :size],
                    preferred_element_type=f32,
                )

    @pl.loop(0, rows // 16)
    def _(step):
        at = pl.ds(pl.multiple_of(step * 16, 16), 16)
        for block in range(width // 128):
            lanes = slice(block * 128, (block + 1) * 128)
            here = [data[chan, at, lanes].astype(f32) for chan in range(2)]
            guess = []
            for chan in range(2):
                rounded = pred_ref[0, chan, at, lanes].astype(bf)
                predb[chan, at, lanes] = rounded
                guess.append(rounded.astype(f32))
            put_terms(at, lanes, here, here, guess)

    @pl.loop(0, runs_len // 16)
    def _(step):
        at = pl.ds(pl.multiple_of(step * 16, 16), 16)
        for block in range(src_rows // 128):
            lanes = slice(block * 128, (block + 1) * 128)
            for chan in range(2):
                mult_ref[0, chan, at, lanes] = (pred_ref[0, chan, at, lanes] * scale).astype(bf)

    for sweep_step in range(SWEEPS - 1):
        box()

        @pl.loop(0, rows // 16)
        def _(step):
            at = pl.ds(pl.multiple_of(step * 16, 16), 16)
            for block in range(width // 128):
                lanes = slice(block * 128, (block + 1) * 128)
                put_terms(at, lanes, *new_err(at, lanes))

    box()

    @pl.loop(0, runs_len // 16)
    def _(step):
        at = pl.ds(pl.multiple_of(step * 16, 16), 16)
        for block in range(src_rows // 128):
            lanes = slice(block * 128, (block + 1) * 128)
            err, _, _ = new_err(at, lanes)
            prim_ref[0, 0, at, lanes] = err[0].astype(bf)
            prim_ref[0, 1, at, lanes] = err[1].astype(bf)


def sweep_call(record, rims, sides, pred, panel):
    _, _, rcv_cols, src_rows = record.shape
    runs, _, rows, width = pred.shape
    run_len = rcv_cols // runs
    f32, bf = jnp.float32, jnp.bfloat16
    out = jax.ShapeDtypeStruct(record.shape, bf)
    tile = pl.BlockSpec((1, 2, run_len, src_rows), lambda r: (0, 0, r, 0))
    return pl.pallas_call(
        functools.partial(sweep_kernel, panel ** (-0.5)),
        grid=(runs,),
        out_shape=(out, out),
        in_specs=[
            tile,
            pl.BlockSpec((2, 1, 2 * HALO, src_rows), lambda r: (0, r, 0, 0)),
            pl.BlockSpec((2, 1, rows, 128), lambda r: (0, r, 0, 0)),
            pl.BlockSpec((1, 2, rows, width), lambda r: (r, 0, 0, 0)),
        ],
        out_specs=(tile, tile),
        scratch_shapes=[
            pltpu.VMEM((2, rows, width), bf),
            pltpu.VMEM((2, rows, width), bf),
            pltpu.VMEM((3, rows, width), bf),
            pltpu.VMEM((3, rows, width + 256), bf),
            pltpu.VMEM((3, rows, width), f32),
            pltpu.VMEM((rows, rows), bf),
            pltpu.VMEM((512, 256), bf),
        ],
        compiler_params=pltpu.CompilerParams(vmem_limit_bytes=56 * 1024 * 1024),
        cost_estimate=pl.CostEstimate(
            flops=12_000_000_000, bytes_accessed=4 * record.size * 2, transcendentals=2 * record.size
        ),
    )(record, rims, sides, pred)


def panel_places(panel_offset, src_count, rcv_count, src_pos, rcv_pos, run_len, src_rows):
    per_run = run_len // STRIDE
    run_ids = jnp.arange(src_count, dtype=jnp.int32)[:, None]
    within = jnp.arange(per_run, dtype=jnp.int32)[None, :]
    per_src = src_rows // STRIDE
    mine = [
        lax.dynamic_slice(panel_offset, (per_src * run + per_run * rcv_pos,), (per_run,))
        for run in range(src_count)
    ]
    col_index = (run_len * run_ids + STRIDE * within).reshape(-1) + jnp.concatenate(mine)
    groups = jnp.arange(per_src, dtype=jnp.int32)
    row_index = STRIDE * groups + lax.dynamic_slice(panel_offset, (per_src * src_pos,), (per_src,))
    return col_index, row_index

def exchange_kernel(
    sizes, rec, col_pick, row_pick, pred, rims, sides,
    front_tx, front_rx, behind_tx, behind_rx, head_tx, head_rx, tail_tx, tail_rx,
    first_tx, after_rx, last_tx, before_rx, own, next_rx, prev_rx, picks, left, right, tiles,
    front_send, front_recv, behind_send, behind_recv, edge_send, edge_recv,
    right_send, right_recv, line_send, left_recv, pair_send, rim_send, rim_recv, out_sem,
):
    srcs, rcvs = sizes
    src = lax.axis_index("src")
    rcv = lax.axis_index("rcv")
    f32, bf = jnp.float32, jnp.bfloat16
    rcv_cols, src_rows = rec.shape[1:]
    run_len = rcv_cols // srcs
    rows = run_len + 2 * HALO
    width = src_rows + 128
    panel = right.shape[3]
    each = panel // (srcs * rcvs)
    spots = rcvs // 2
    spot, core = rcv // 2, lax.rem(rcv, 2)

    def remote(source, target, send, recv, where):
        return pltpu.make_async_remote_copy(
            src_ref=source, dst_ref=target, send_sem=send, recv_sem=recv,
            device_id=where, device_id_type=MESH,
        )

    rcv_peers = [lax.rem(rcv + step, rcvs) for step in range(1, rcvs)]
    src_peers = [lax.rem(src + step, srcs) for step in range(1, srcs)]
    last_rcv, first_rcv = rcv == rcvs - 1, rcv == 0
    has_next = jnp.logical_not(jnp.logical_and(last_rcv, src == srcs - 1))
    has_prev = jnp.logical_not(jnp.logical_and(first_rcv, src == 0))
    next_dev = (
        jnp.where(last_rcv, jnp.minimum(src + 1, srcs - 1), src), jnp.where(last_rcv, 0, rcv + 1)
    )
    prev_dev = (
        jnp.where(first_rcv, jnp.maximum(src - 1, 0), src), jnp.where(first_rcv, rcvs - 1, rcv - 1)
    )
    far_next = jnp.logical_and(last_rcv, src < srcs - 1)
    far_prev = jnp.logical_and(first_rcv, src > 0)

    left[src_rows:] = jnp.zeros((128, 2 * panel), bf)
    barrier = pltpu.get_barrier_semaphore()
    for peer in rcv_peers:
        pl.semaphore_signal(barrier, inc=1, device_id=(src, peer), device_id_type=MESH)
    for peer in src_peers:
        pl.semaphore_signal(barrier, inc=1, device_id=(peer, rcv), device_id_type=MESH)

    @pl.when(far_next)
    def _():
        pl.semaphore_signal(barrier, inc=1, device_id=next_dev, device_id_type=MESH)

    @pl.when(far_prev)
    def _():
        pl.semaphore_signal(barrier, inc=1, device_id=prev_dev, device_id_type=MESH)

    for chan in range(2):
        for pair in range(srcs // 2):
            for buffer, start in ((head_tx, 0), (tail_tx, run_len - 16)):
                ends = [
                    rec[chan, run * run_len + start : run * run_len + start + 16].astype(f32)
                    for run in (2 * pair, 2 * pair + 1)
                ]
                part = slice(0, HALO) if start == 0 else slice(16 - HALO, 16)
                buffer[chan, 16 * pair : 16 * pair + 16] = jnp.concatenate(
                    [end[part] for end in ends], axis=0
                ).astype(bf)

    pl.semaphore_wait(
        barrier,
        rcvs - 1 + srcs - 1 + jnp.where(far_next, 1, 0) + jnp.where(far_prev, 1, 0),
    )
    heads = remote(
        head_tx, head_rx, edge_send.at[0], edge_recv.at[0], (src, lax.rem(rcv + rcvs - 1, rcvs))
    )
    tails = remote(tail_tx, tail_rx, edge_send.at[1], edge_recv.at[1], (src, lax.rem(rcv + 1, rcvs)))
    heads.start()
    tails.start()

    fronts, behinds = [], []
    for chan in range(2):
        picked = lax.dot_general(
            rec[chan], col_pick[...], (((0,), (0,)), ((), ())), preferred_element_type=f32
        ).astype(bf)
        for peer in range(rcvs):
            front_tx[peer, chan] = picked[peer * run_len : (peer + 1) * run_len]
        for index, peer in enumerate(rcv_peers):
            copy = remote(
                front_tx.at[peer, chan], front_rx.at[rcv, chan], front_send.at[chan, index],
                front_recv.at[chan, rcv], (src, peer),
            )
            copy.start()
            fronts.append(copy)
        front_rx[rcv, chan] = front_tx[rcv, chan]
    for chan in range(2):
        picked = jnp.dot(rec[chan], row_pick[...], preferred_element_type=f32).astype(bf)
        for peer in range(srcs):
            behind_tx[peer, chan] = picked[peer * run_len : (peer + 1) * run_len]
        for index, peer in enumerate(src_peers):
            copy = remote(
                behind_tx.at[peer, chan], behind_rx.at[src, chan], behind_send.at[chan, index],
                behind_recv.at[chan, src], (peer, rcv),
            )
            copy.start()
            behinds.append(copy)
        behind_rx[src, chan] = behind_tx[src, chan]

    keys = srcs * each
    for peer in range(rcvs):
        index = lax.broadcasted_iota(jnp.int32, (keys, panel), 0)
        column = lax.broadcasted_iota(jnp.int32, (keys, panel), 1)
        aim = index // each * (rcvs * each) + peer * each + index % each
        picks[peer * keys : (peer + 1) * keys] = jnp.where(column == aim, 1.0, 0.0).astype(bf)

    heads.wait()
    tails.wait()

    def edge(buffer, chan, run):
        if run < 0 or run >= srcs:
            return jnp.zeros((HALO, src_rows), f32)
        tile = buffer[chan, run // 2 * 16 : run // 2 * 16 + 16].astype(f32)
        return tile[run % 2 * HALO : run % 2 * HALO + HALO]

    for chan in range(2):
        for run in range(srcs):
            below = jnp.where(last_rcv, edge(head_rx, chan, run + 1), edge(head_rx, chan, run))
            above = jnp.where(first_rcv, edge(tail_rx, chan, run - 1), edge(tail_rx, chan, run))
            rim = jnp.concatenate([below, above], axis=0).astype(bf)
            rims[chan, run] = rim
            main = slice(run * run_len, (run + 1) * run_len)
            first_tx[chan, run, :run_len] = rec[chan, main, :128]
            first_tx[chan, run, run_len:] = rim[:, :128]
            last_tx[chan, run, :run_len] = rec[chan, main, src_rows - 128 :]
            last_tx[chan, run, run_len:] = rim[:, src_rows - 128 :]

    low = jnp.maximum(src - 1, 0)
    high = jnp.minimum(src + 1, srcs - 1)
    firsts = remote(first_tx, after_rx, edge_send.at[2], edge_recv.at[2], (low, rcv))
    lasts = remote(last_tx, before_rx, edge_send.at[3], edge_recv.at[3], (high, rcv))

    @pl.when(src > 0)
    def _():
        firsts.start()

    @pl.when(src < srcs - 1)
    def _():
        lasts.start()

    def line(owner_spot, source, up, step, chan):
        owner = 2 * owner_spot + core
        shift = 2 if up else -2
        return remote(
            source, shard(owner, chan), line_send.at[chan, 0 if up else 1, step],
            left_recv.at[chan, owner], (src, jnp.clip(rcv + shift, 0, rcvs - 1)),
        )

    def hand(owner, source, chan):
        return remote(
            source, shard(owner, chan), pair_send.at[chan, owner // 2], left_recv.at[chan, owner],
            (src, rcv + 1 - 2 * core),
        )

    def shard(owner, chan):
        return left.at[
            pl.ds(pl.multiple_of(owner * run_len, 16), run_len), pl.ds(chan * panel, panel)
        ]

    to_prev, to_next = [], []
    for chan in range(2):
        for index, step in enumerate(range(1, rcvs)):
            peer = lax.rem(rcv + rcvs - step, rcvs)
            remote(
                front_tx.at[peer, chan], front_rx.at[peer, chan], front_send.at[chan, index],
                front_recv.at[chan, peer], (src, peer),
            ).wait_recv()
        for index, step in enumerate(range(1, srcs)):
            peer = lax.rem(src + srcs - step, srcs)
            remote(
                behind_tx.at[peer, chan], behind_rx.at[peer, chan], behind_send.at[chan, index],
                behind_recv.at[chan, peer], (peer, rcv),
            ).wait_recv()
        total = jnp.zeros((run_len, panel), f32)
        for peer in range(rcvs):
            total = total + jnp.dot(
                front_rx[peer, chan], picks[peer * keys : (peer + 1) * keys],
                preferred_element_type=f32,
            )
        for peer in range(srcs):
            shape = (rcvs * each, panel)
            index = lax.broadcasted_iota(jnp.int32, shape, 0)
            column = lax.broadcasted_iota(jnp.int32, shape, 1)
            pick = jnp.where(column == index + peer * rcvs * each, 1.0, 0.0).astype(bf)
            total = total + jnp.dot(behind_rx[peer, chan], pick, preferred_element_type=f32)
        own[chan, :run_len] = (total * 0.5).astype(bf)
        mine = own.at[chan, pl.ds(0, run_len)]

        @pl.when(spot < spots - 1)
        def _():
            line(spot, mine, True, 0, chan).start()

        @pl.when(spot > 0)
        def _():
            line(spot, mine, False, 0, chan).start()

        hand(rcv, mine, chan).start()
        to_prev.append(
            remote(
                own.at[chan, pl.ds(0, 16)], next_rx.at[chan], edge_send.at[4 + chan],
                edge_recv.at[4 + chan], prev_dev,
            )
        )
        to_next.append(
            remote(
                own.at[chan, pl.ds(run_len - 16, 16)], prev_rx.at[chan], edge_send.at[6 + chan],
                edge_recv.at[6 + chan], next_dev,
            )
        )

        @pl.when(has_prev)
        def _():
            to_prev[chan].start()

        @pl.when(has_next)
        def _():
            to_next[chan].start()

        left[
            pl.ds(pl.multiple_of(rcv * run_len, 16), run_len), chan * panel : (chan + 1) * panel
        ] = own[chan, :run_len]

    @pl.when(has_next)
    def _():
        for chan in range(2):
            to_prev[chan].wait_recv()

    @pl.when(jnp.logical_not(has_next))
    def _():
        next_rx[...] = jnp.zeros_like(next_rx)

    @pl.when(has_prev)
    def _():
        for chan in range(2):
            to_next[chan].wait_recv()

    @pl.when(jnp.logical_not(has_prev))
    def _():
        prev_rx[...] = jnp.zeros_like(prev_rx)

    place = lax.broadcasted_iota(jnp.int32, (2, 2 * HALO, panel), 1)
    own[:, run_len:] = jnp.where(place < HALO, next_rx[...], prev_rx[...])
    rights = []
    for index, peer in enumerate(src_peers):
        copy = remote(own, right.at[src], right_send.at[index], right_recv.at[src], (peer, rcv))
        copy.start()
        rights.append(copy)
    right[src] = own[...]

    def rim_copy(start, chan, index, which, peer):
        return remote(
            own.at[chan, pl.ds(run_len, 2 * HALO)],
            left.at[pl.ds(start, 2 * HALO), pl.ds(chan * panel, panel)],
            rim_send.at[chan, index], rim_recv.at[chan, which], (src, peer),
        )

    rim_ends = ((first_rcv, width - 2 * HALO, 0), (last_rcv, src_rows, 1))
    for holds, start, which in rim_ends:

        @pl.when(holds)
        def _():
            for chan in range(2):
                for index, peer in enumerate(rcv_peers):
                    rim_copy(start, chan, index, which, peer).start()
                left[start : start + 2 * HALO, chan * panel : (chan + 1) * panel] = own[
                    chan, run_len:
                ]

    def multiply(start, size):
        @pl.loop(0, srcs)
        def _(run):
            at = pl.ds(start, size)
            left_real = left[at, :panel]
            left_imag = left[at, panel:]
            contract = (((1,), (1,)), ((), ()))

            def dot(one, two):
                return lax.dot_general(one, two, contract, preferred_element_type=f32)

            right_real = right[run, 0]
            right_imag = right[run, 1]
            tiles[run, 0, :, at] = dot(right_real, left_real) - dot(right_imag, left_imag)
            tiles[run, 1, :, at] = dot(right_real, left_imag) + dot(right_imag, left_real)

    def out_copy(start, size, index):
        return pltpu.make_async_copy(
            tiles.at[:, :, :, pl.ds(start, size)],
            pred.at[:, :, :, pl.ds(start, size)],
            out_sem.at[index],
        )

    span = 2 * run_len

    def tile_of(owner_spot):
        for chan in range(2):
            hand(2 * owner_spot + 1 - core, shard(rcv, chan), chan).wait_recv()
        start = pl.multiple_of(owner_spot * span, 128)
        multiply(start, span)
        out_copy(start, span, owner_spot).start()

    def tiles_at(step):
        if step == 0:
            tile_of(spot)
            return

        @pl.when(spot >= step)
        def _():
            tile_of(spot - step)

        @pl.when(spot + step < spots)
        def _():
            tile_of(spot + step)

    for step in range(1, spots):
        if step == spots - 1:
            for other in range(1, srcs):
                peer = lax.rem(src + srcs - other, srcs)
                remote(
                    own, right.at[peer], right_send.at[0], right_recv.at[peer], (peer, rcv)
                ).wait_recv()
            for done in range(spots - 1):
                tiles_at(done)
        for chan in range(2):
            for up in (True, False):
                owner_spot = spot - step if up else spot + step
                arrives = spot >= step if up else spot + step < spots
                onward = spot < spots - 1 if up else spot > 0

                @pl.when(arrives)
                def _():
                    owner = 2 * owner_spot + core
                    block = shard(owner, chan)
                    line(owner_spot, block, up, step - 1, chan).wait_recv()
                    if step < spots - 1:

                        @pl.when(onward)
                        def _():
                            line(owner_spot, block, up, step, chan).start()

                    hand(owner, block, chan).start()

    for holds, start, which in rim_ends:

        @pl.when(jnp.logical_not(holds))
        def _():
            for chan in range(2):
                rim_copy(start, chan, 0, which, rcv).wait_recv()

    multiply(src_rows, 128)
    out_copy(src_rows, 128, spots).start()
    tiles_at(spots - 1)

    for copy in fronts + behinds:
        copy.wait_send()

    @pl.when(src > 0)
    def _():
        firsts.wait_send()
        lasts.wait_recv()

    @pl.when(src < srcs - 1)
    def _():
        lasts.wait_send()
        firsts.wait_recv()

    @pl.when(src == 0)
    def _():
        before_rx[...] = jnp.zeros_like(before_rx)

    @pl.when(src == srcs - 1)
    def _():
        after_rx[...] = jnp.zeros_like(after_rx)

    lane = lax.broadcasted_iota(jnp.int32, (rows, 128), 1)
    zero = jnp.zeros((rows, 128), bf)
    for chan in range(2):
        for run in range(srcs):
            sides[chan, run] = jnp.where(
                lane < HALO, after_rx[chan, run], jnp.where(lane >= 128 - HALO, before_rx[chan, run], zero)
            )

    for chan in range(2):

        @pl.when(has_prev)
        def _():
            to_prev[chan].wait_send()

        @pl.when(has_next)
        def _():
            to_next[chan].wait_send()

        for holds, start, which in rim_ends:

            @pl.when(holds)
            def _():
                for index, peer in enumerate(rcv_peers):
                    rim_copy(start, chan, index, which, peer).wait_send()

        mine = own.at[chan, pl.ds(0, run_len)]
        for step in range(spots - 1):

            @pl.when(jnp.logical_and(spot < spots - 1, spot >= step))
            def _():
                line(spot, mine, True, step, chan).wait_send()

            @pl.when(jnp.logical_and(spot > 0, spot + step < spots))
            def _():
                line(spot, mine, False, step, chan).wait_send()

        for index in range(spots):
            hand(2 * index + core, mine, chan).wait_send()

    for copy in rights:
        copy.wait_send()
    for index in range(spots):
        out_copy(index * span, span, index).wait()
    out_copy(src_rows, 128, spots).wait()


def exchange_call(rec, col_pick, row_pick, srcs, rcvs, panel):
    _, rcv_cols, src_rows = rec.shape
    run_len = rcv_cols // srcs
    rows = run_len + 2 * HALO
    bf = jnp.bfloat16
    vmem = pl.BlockSpec(memory_space=pltpu.VMEM)
    front = (rcvs, 2, run_len, col_pick.shape[1])
    behind = (srcs, 2, run_len, row_pick.shape[1])
    edges = (2, HALO * srcs, src_rows)
    side = (2, srcs, rows, 128)
    shapes = [front, front, behind, behind, edges, edges, edges, edges, side, side, side, side]
    shapes += [(2, rows, panel), (2, 16, panel), (2, 16, panel), (panel, panel)]
    shapes += [(src_rows + 128, 2 * panel), (srcs, 2, rows, panel)]
    wide = (srcs, 2, rows, src_rows + 128)
    dma = pltpu.SemaphoreType.DMA
    return pl.pallas_call(
        functools.partial(exchange_kernel, (srcs, rcvs)),
        out_shape=(
            jax.ShapeDtypeStruct(wide, jnp.float32),
            jax.ShapeDtypeStruct((2, srcs, 2 * HALO, src_rows), bf),
            jax.ShapeDtypeStruct(side, bf),
        ),
        in_specs=[vmem] * 3,
        out_specs=(pl.BlockSpec(memory_space=pl.ANY), vmem, vmem),
        scratch_shapes=[pltpu.VMEM(shape, bf) for shape in shapes]
        + [pltpu.VMEM(wide, jnp.float32)]
        + [
            dma((2, rcvs)), dma((2, rcvs)), dma((2, srcs)), dma((2, srcs)), dma((8,)), dma((8,)),
            dma((srcs,)), dma((srcs,)), dma((2, 2, rcvs // 2)), dma((2, rcvs)), dma((2, rcvs // 2)),
            dma((2, rcvs)), dma((2, 2)), dma((rcvs // 2 + 1,)),
        ],
        compiler_params=pltpu.CompilerParams(
            collective_id=0, has_side_effects=True, vmem_limit_bytes=56 * 1024 * 1024
        ),
        cost_estimate=pl.CostEstimate(
            flops=10_000_000_000, bytes_accessed=8 * rec.size, transcendentals=0
        ),
    )(rec, col_pick, row_pick)


def shards(record, panel_offset):
    src_count = lax.axis_size("src")
    rcv_count = lax.axis_size("rcv")
    freqs, _, rcv_cols, src_rows = record.shape
    run_len = rcv_cols // src_count
    if freqs != 1 or run_len % 16 or src_rows % 128 or src_count % 2 or rcv_count % 2 or run_len % 64 or rcv_count < 4:
        return plain_shards(record, panel_offset)
    src_pos = lax.axis_index("src")
    rcv_pos = lax.axis_index("rcv")
    panel = panel_offset.shape[0]
    col_index, row_index = panel_places(
        panel_offset, src_count, rcv_count, src_pos, rcv_pos, run_len, src_rows
    )
    rec = record[0]
    col_pick = (jnp.arange(rcv_cols)[:, None] == col_index[None, :]).astype(record.dtype)
    row_pick = (jnp.arange(src_rows)[:, None] == row_index[None, :]).astype(record.dtype)
    pred, rims, sides = exchange_call(rec, col_pick, row_pick, src_count, rcv_count, panel)
    return sweep_call(record, rims, sides, pred, panel)


def solution(mesh):
    in_specs = (P(None, None, "rcv", "src"), P())
    out_specs = (P(None, None, "rcv", "src"), P(None, None, "rcv", "src"))
    return jax.shard_map(shards, mesh=mesh, in_specs=in_specs, out_specs=out_specs, check_vma=False)
```

```python
import functools

import jax
import jax.numpy as jnp
from jax import lax
from jax.experimental import pallas as pl
from jax.experimental.pallas import tpu as pltpu
from jax.sharding import PartitionSpec as P

STRIDE = 8
REACH = 4
SWEEPS = 2


weight_eps = 1e-06


def extended(cells, sides, width, closed):
    for axis, dim in sides:
        count = lax.axis_size(axis)
        ends = count if closed else count - 1
        head = lax.slice_in_dim(cells, 0, width, axis=dim)
        tail = lax.slice_in_dim(cells, cells.shape[dim] - width, cells.shape[dim], axis=dim)
        cells = jnp.concatenate(
            [
                lax.ppermute(tail, axis, [(i, (i + 1) % count) for i in range(ends)]),
                cells,
                lax.ppermute(head, axis, [((i + 1) % count, i) for i in range(ends)]),
            ],
            axis=dim,
        )
    return cells


def reorder_keys(values, rcv_count, src_count):
    full_shape = values.shape
    grouped = values.reshape(
        full_shape[:-1] + (rcv_count, src_count, full_shape[-1] // (rcv_count * src_count))
    )
    return jnp.swapaxes(grouped, -3, -2).reshape(full_shape)


def average_pair(first_part, second_part):
    return ((first_part.astype(jnp.float32) + second_part.astype(jnp.float32)) * 0.5).astype(
        jnp.bfloat16
    )


def cross_dot(left_mat, right_mat):
    return lax.dot_general(
        left_mat, right_mat, (((2,), (2,)), ((0,), (0,))), preferred_element_type=jnp.float32
    )


def predict_block(right_side, left_side):
    right_real = right_side[:, 0]
    right_imag = right_side[:, 1]
    left_real = left_side[:, 0]
    left_imag = left_side[:, 1]
    pred_real = cross_dot(right_real, left_real) - cross_dot(right_imag, left_imag)
    pred_imag = cross_dot(right_real, left_imag) + cross_dot(right_imag, left_real)
    return jnp.stack([pred_real, pred_imag], axis=1)


def neighbour_sum(partial_terms, src_count, rcv_pos, rcv_count):
    freq_count, chan_count, rcv_cols, src_rows = partial_terms.shape
    run_len = rcv_cols // src_count
    runs_view = partial_terms.reshape(freq_count, chan_count, src_count, run_len, src_rows)
    padded = extended(runs_view.astype(jnp.bfloat16), (("rcv", 3),), REACH, True).astype(
        runs_view.dtype
    )
    lower_rim = padded[:, :, :, :REACH]
    middle = padded[:, :, :, REACH : REACH + run_len]
    upper_rim = padded[:, :, :, REACH + run_len :]
    zero_rim = jnp.zeros_like(lower_rim[:, :, :1])
    lower_rim = jnp.where(
        rcv_pos == 0, jnp.concatenate([zero_rim, lower_rim[:, :, :-1]], axis=2), lower_rim
    )
    upper_rim = jnp.where(
        rcv_pos == rcv_count - 1,
        jnp.concatenate([upper_rim[:, :, 1:], zero_rim], axis=2),
        upper_rim,
    )
    padded = jnp.concatenate([lower_rim, middle, upper_rim], axis=3)
    recv_total = padded[:, :, :, 0:run_len]
    for shift_pos in range(1, 2 * REACH + 1):
        recv_total = recv_total + padded[:, :, :, shift_pos : shift_pos + run_len]
    recv_total = recv_total.reshape(freq_count, chan_count, rcv_cols, src_rows)
    src_padded = extended(recv_total.astype(jnp.bfloat16), (("src", 3),), REACH, False).astype(
        recv_total.dtype
    )
    box_totals = src_padded[..., 0:src_rows]
    for shift_pos in range(1, 2 * REACH + 1):
        box_totals = box_totals + src_padded[..., shift_pos : shift_pos + src_rows]
    return box_totals


def run_sweeps(data_bf, pred_bf, summer):
    data_f32 = data_bf.astype(jnp.float32)
    pred_f32 = pred_bf.astype(jnp.float32)
    data_real = data_f32[:, 0]
    data_imag = data_f32[:, 1]
    pred_real = pred_f32[:, 0]
    pred_imag = pred_f32[:, 1]
    err_real = data_real
    err_imag = data_imag
    for sweep_step in range(SWEEPS):
        weight = 1.5 - jnp.tanh(err_real * err_real + err_imag * err_imag)
        partial_terms = jnp.stack(
            [
                weight * (pred_real * data_real + pred_imag * data_imag),
                weight * (pred_real * data_imag - pred_imag * data_real),
                weight * (pred_real * pred_real + pred_imag * pred_imag),
            ],
            axis=1,
        )
        box_totals = summer(partial_terms)
        denom = box_totals[:, 2] + weight_eps
        gain_real = box_totals[:, 0] / denom
        gain_imag = box_totals[:, 1] / denom
        err_real = data_real - (gain_real * pred_real - gain_imag * pred_imag)
        err_imag = data_imag - (gain_real * pred_imag + gain_imag * pred_real)
    return jnp.stack([err_real, err_imag], axis=1)


def plain_shards(record, panel_offset):
    src_count = lax.axis_size("src")
    rcv_count = lax.axis_size("rcv")
    src_pos = lax.axis_index("src")
    rcv_pos = lax.axis_index("rcv")
    rcv_cols = record.shape[2]
    src_rows = record.shape[3]
    run_len = rcv_cols // src_count
    per_run = run_len // STRIDE
    panel_len = panel_offset.shape[0]
    run_ids = jnp.arange(src_count, dtype=jnp.int32)[:, None]
    within = jnp.arange(per_run, dtype=jnp.int32)[None, :]
    col_groups = (src_rows * run_ids + run_len * rcv_pos) // STRIDE + within
    col_index = (run_len * run_ids + STRIDE * within + jnp.take(panel_offset, col_groups)).reshape(
        -1
    )
    row_groups = jnp.arange(src_rows // STRIDE, dtype=jnp.int32)
    row_index = STRIDE * row_groups + jnp.take(
        panel_offset, src_rows // STRIDE * src_pos + row_groups
    )
    col_piece = jnp.swapaxes(jnp.take(record, col_index, axis=2), 2, 3)
    row_piece = jnp.take(record, row_index, axis=3)
    own_front = reorder_keys(
        lax.all_to_all(col_piece, "rcv", split_axis=2, concat_axis=3, tiled=True),
        rcv_count,
        src_count,
    )
    own_behind = lax.all_to_all(row_piece, "src", split_axis=2, concat_axis=3, tiled=True)
    owned_rows = average_pair(own_front, own_behind)
    right_side = lax.all_gather(owned_rows, "src", axis=2, tiled=True)
    prediction = predict_block(right_side, lax.all_gather(owned_rows, "rcv", axis=2, tiled=True))
    pred_round = lax.optimization_barrier(prediction.astype(jnp.bfloat16))
    multiples = (prediction * panel_len ** (-0.5)).astype(jnp.bfloat16)

    def runs_total(partial_terms):
        return neighbour_sum(partial_terms, src_count, rcv_pos, rcv_count)

    primaries = run_sweeps(record, pred_round, runs_total).astype(jnp.bfloat16)
    return (primaries, multiples)

HALO = 2 * REACH
MESH = pl.DeviceIdType.MESH


def wide_spans(width):
    spans = [(start, 256) for start in range(0, width - 255, 256)]
    done = 256 * (width // 256)
    return spans + ([(done, width - done)] if done < width else [])


def band(shape, shift, period):
    rows = lax.broadcasted_iota(jnp.int32, shape, 0)
    cols = lax.broadcasted_iota(jnp.int32, shape, 1) + shift
    gap = jnp.abs(rows - cols)
    if period:
        gap = jnp.minimum(gap, period - gap)
    return jnp.where(gap <= REACH, 1.0, 0.0).astype(jnp.bfloat16)


def sweep_kernel(
    scale, record_ref, rim_ref, side_ref, pred_ref, prim_ref, mult_ref,
    data, predb, terms, partial, totals, row_band, lane_band
):
    runs_len = record_ref.shape[2]
    src_rows = record_ref.shape[3]
    rows = runs_len + 2 * HALO
    width = src_rows + 128
    f32, bf = jnp.float32, jnp.bfloat16

    @pl.when(pl.program_id(0) == 0)
    def _():
        row_band[...] = band((rows, rows), 0, rows)
        lane_band[...] = band((512, 256), 128, 0)

    for chan in range(2):
        data[chan, :runs_len, :src_rows] = record_ref[0, chan]
        data[chan, runs_len:, :src_rows] = rim_ref[chan, 0]
        data[chan, :, src_rows:] = side_ref[chan, 0]

    def put_terms(at, lanes, err, here, guess):
        weight = 1.5 - jnp.tanh(err[0] * err[0] + err[1] * err[1])
        parts = (
            guess[0] * here[0] + guess[1] * here[1],
            guess[0] * here[1] - guess[1] * here[0],
            guess[0] * guess[0] + guess[1] * guess[1],
        )
        for index, part in enumerate(parts):
            terms[index, at, lanes] = (weight * part).astype(bf)

    def new_err(at, lanes):
        here = [data[chan, at, lanes].astype(f32) for chan in range(2)]
        guess = [predb[chan, at, lanes].astype(f32) for chan in range(2)]
        inverse = 1.0 / (totals[2, at, lanes] + weight_eps)
        gain_real = totals[0, at, lanes] * inverse
        gain_imag = totals[1, at, lanes] * inverse
        err = (
            here[0] - (gain_real * guess[0] - gain_imag * guess[1]),
            here[1] - (gain_real * guess[1] + gain_imag * guess[0]),
        )
        return err, here, guess

    def box():
        for index in range(3):
            for start, size in wide_spans(width):
                partial[index, :, 128 + start : 128 + start + size] = jnp.dot(
                    row_band[...], terms[index, :, start : start + size], preferred_element_type=f32
                ).astype(bf)
            partial[index, :, :128] = partial[index, :, width : width + 128]
            partial[index, :, width + 128 :] = partial[index, :, 128:256]
        for index in range(3):
            for start, size in wide_spans(width):
                totals[index, :, start : start + size] = jnp.dot(
                    partial[index, :, start : start + size + 256],
                    lane_band[: size + 256, :size],
                    preferred_element_type=f32,
                )

    @pl.loop(0, rows // 16)
    def _(step):
        at = pl.ds(pl.multiple_of(step * 16, 16), 16)
        for block in range(width // 128):
            lanes = slice(block * 128, (block + 1) * 128)
            here = [data[chan, at, lanes].astype(f32) for chan in range(2)]
            guess = []
            for chan in range(2):
                rounded = pred_ref[chan, 0, at, lanes].astype(bf)
                predb[chan, at, lanes] = rounded
                guess.append(rounded.astype(f32))
            put_terms(at, lanes, here, here, guess)

    @pl.loop(0, runs_len // 16)
    def _(step):
        at = pl.ds(pl.multiple_of(step * 16, 16), 16)
        for block in range(src_rows // 128):
            lanes = slice(block * 128, (block + 1) * 128)
            for chan in range(2):
                mult_ref[0, chan, at, lanes] = (pred_ref[chan, 0, at, lanes] * scale).astype(bf)

    for sweep_step in range(SWEEPS - 1):
        box()

        @pl.loop(0, rows // 16)
        def _(step):
            at = pl.ds(pl.multiple_of(step * 16, 16), 16)
            for block in range(width // 128):
                lanes = slice(block * 128, (block + 1) * 128)
                put_terms(at, lanes, *new_err(at, lanes))

    box()

    @pl.loop(0, runs_len // 16)
    def _(step):
        at = pl.ds(pl.multiple_of(step * 16, 16), 16)
        for block in range(src_rows // 128):
            lanes = slice(block * 128, (block + 1) * 128)
            err, _, _ = new_err(at, lanes)
            prim_ref[0, 0, at, lanes] = err[0].astype(bf)
            prim_ref[0, 1, at, lanes] = err[1].astype(bf)


def sweep_call(record, rims, sides, pred, panel):
    _, _, rcv_cols, src_rows = record.shape
    _, runs, rows, width = pred.shape
    run_len = rcv_cols // runs
    f32, bf = jnp.float32, jnp.bfloat16
    out = jax.ShapeDtypeStruct(record.shape, bf)
    tile = pl.BlockSpec((1, 2, run_len, src_rows), lambda r: (0, 0, r, 0))
    return pl.pallas_call(
        functools.partial(sweep_kernel, panel ** (-0.5)),
        grid=(runs,),
        out_shape=(out, out),
        in_specs=[
            tile,
            pl.BlockSpec((2, 1, 2 * HALO, src_rows), lambda r: (0, r, 0, 0)),
            pl.BlockSpec((2, 1, rows, 128), lambda r: (0, r, 0, 0)),
            pl.BlockSpec((2, 1, rows, width), lambda r: (0, r, 0, 0)),
        ],
        out_specs=(tile, tile),
        scratch_shapes=[
            pltpu.VMEM((2, rows, width), bf),
            pltpu.VMEM((2, rows, width), bf),
            pltpu.VMEM((3, rows, width), bf),
            pltpu.VMEM((3, rows, width + 256), bf),
            pltpu.VMEM((3, rows, width), f32),
            pltpu.VMEM((rows, rows), bf),
            pltpu.VMEM((512, 256), bf),
        ],
        compiler_params=pltpu.CompilerParams(vmem_limit_bytes=56 * 1024 * 1024),
        cost_estimate=pl.CostEstimate(
            flops=12_000_000_000, bytes_accessed=4 * record.size * 2, transcendentals=2 * record.size
        ),
    )(record, rims, sides, pred)


def exchange_kernel(
    sizes, rec, offset, pred, rims, sides,
    front_tx, front_rx, behind_tx, behind_rx, head_tx, head_rx, tail_tx, tail_rx,
    first_tx, after_rx, last_tx, before_rx, own, next_rx, prev_rx, picks, left, right, right_all, tiles,
    col_pick, row_pick,
    front_send, front_recv, behind_send, behind_recv, edge_send, edge_recv,
    right_send, right_recv, line_send, left_recv, pair_send, rim_send, rim_recv, out_sem,
):
    srcs, rcvs = sizes
    src = lax.axis_index("src")
    rcv = lax.axis_index("rcv")
    f32, bf = jnp.float32, jnp.bfloat16
    rcv_cols, src_rows = rec.shape[1:]
    run_len = rcv_cols // srcs
    rows = run_len + 2 * HALO
    width = src_rows + 128
    panel = right.shape[3]
    each = panel // (srcs * rcvs)
    spots = rcvs // 2
    spot, core = rcv // 2, lax.rem(rcv, 2)

    def remote(source, target, send, recv, where):
        return pltpu.make_async_remote_copy(
            src_ref=source, dst_ref=target, send_sem=send, recv_sem=recv,
            device_id=where, device_id_type=MESH,
        )

    rcv_peers = [lax.rem(rcv + step, rcvs) for step in range(1, rcvs)]
    src_peers = [lax.rem(src + step, srcs) for step in range(1, srcs)]
    last_rcv, first_rcv = rcv == rcvs - 1, rcv == 0
    has_next = jnp.logical_not(jnp.logical_and(last_rcv, src == srcs - 1))
    has_prev = jnp.logical_not(jnp.logical_and(first_rcv, src == 0))
    next_dev = (
        jnp.where(last_rcv, jnp.minimum(src + 1, srcs - 1), src), jnp.where(last_rcv, 0, rcv + 1)
    )
    prev_dev = (
        jnp.where(first_rcv, jnp.maximum(src - 1, 0), src), jnp.where(first_rcv, rcvs - 1, rcv - 1)
    )
    far_next = jnp.logical_and(last_rcv, src < srcs - 1)
    far_prev = jnp.logical_and(first_rcv, src > 0)

    left[src_rows:] = jnp.zeros((128, 2 * panel), bf)
    barrier = pltpu.get_barrier_semaphore()
    for peer in rcv_peers:
        pl.semaphore_signal(barrier, inc=1, device_id=(src, peer), device_id_type=MESH)
    for peer in src_peers:
        pl.semaphore_signal(barrier, inc=1, device_id=(peer, rcv), device_id_type=MESH)

    @pl.when(far_next)
    def _():
        pl.semaphore_signal(barrier, inc=1, device_id=next_dev, device_id_type=MESH)

    @pl.when(far_prev)
    def _():
        pl.semaphore_signal(barrier, inc=1, device_id=prev_dev, device_id_type=MESH)

    offsets = jnp.broadcast_to(offset[...].astype(f32), (8, panel)).astype(bf)

    def pick_from(target, count, group_of, cell_of):
        groups = lax.broadcasted_iota(jnp.int32, (panel, count), 0)
        column = lax.broadcasted_iota(jnp.int32, (panel, count), 1)
        chosen = jnp.where(groups == group_of(column), 1.0, 0.0).astype(bf)
        mine = jnp.dot(offsets, chosen, preferred_element_type=f32)[:1].astype(jnp.int32)
        cells = lax.broadcasted_iota(jnp.int32, target.shape, 0)
        column = lax.broadcasted_iota(jnp.int32, (1, count), 1)
        target[...] = jnp.where(cells == cell_of(column) + mine, 1.0, 0.0).astype(bf)

    per_src = rcvs * each
    pick_from(
        col_pick, srcs * each,
        lambda j: j // each * per_src + each * rcv + j % each,
        lambda j: j // each * run_len + STRIDE * (j % each),
    )
    pick_from(row_pick, per_src, lambda j: per_src * src + j, lambda j: STRIDE * j)

    for chan in range(2):
        for pair in range(srcs // 2):
            for buffer, start in ((head_tx, 0), (tail_tx, run_len - 16)):
                ends = [
                    rec[chan, run * run_len + start : run * run_len + start + 16].astype(f32)
                    for run in (2 * pair, 2 * pair + 1)
                ]
                part = slice(0, HALO) if start == 0 else slice(16 - HALO, 16)
                buffer[chan, 16 * pair : 16 * pair + 16] = jnp.concatenate(
                    [end[part] for end in ends], axis=0
                ).astype(bf)

    pl.semaphore_wait(
        barrier,
        rcvs - 1 + srcs - 1 + jnp.where(far_next, 1, 0) + jnp.where(far_prev, 1, 0),
    )
    heads = remote(
        head_tx, head_rx, edge_send.at[0], edge_recv.at[0], (src, lax.rem(rcv + rcvs - 1, rcvs))
    )
    tails = remote(tail_tx, tail_rx, edge_send.at[1], edge_recv.at[1], (src, lax.rem(rcv + 1, rcvs)))
    heads.start()
    tails.start()

    fronts, behinds = [], []
    for chan in range(2):
        picked = lax.dot_general(
            rec[chan], col_pick[...], (((0,), (0,)), ((), ())), preferred_element_type=f32
        ).astype(bf)
        for peer in range(rcvs):
            front_tx[peer, chan] = picked[peer * run_len : (peer + 1) * run_len]
        for index, peer in enumerate(rcv_peers):
            copy = remote(
                front_tx.at[peer, chan], front_rx.at[rcv, chan], front_send.at[chan, index],
                front_recv.at[chan, rcv], (src, peer),
            )
            copy.start()
            fronts.append(copy)
        front_rx[rcv, chan] = front_tx[rcv, chan]
    for chan in range(2):
        picked = jnp.dot(rec[chan], row_pick[...], preferred_element_type=f32).astype(bf)
        for peer in range(srcs):
            behind_tx[peer, chan] = picked[peer * run_len : (peer + 1) * run_len]
        for index, peer in enumerate(src_peers):
            copy = remote(
                behind_tx.at[peer, chan], behind_rx.at[src, chan], behind_send.at[chan, index],
                behind_recv.at[chan, src], (peer, rcv),
            )
            copy.start()
            behinds.append(copy)
        behind_rx[src, chan] = behind_tx[src, chan]

    keys = srcs * each
    for peer in range(rcvs):
        index = lax.broadcasted_iota(jnp.int32, (keys, panel), 0)
        column = lax.broadcasted_iota(jnp.int32, (keys, panel), 1)
        aim = index // each * (rcvs * each) + peer * each + index % each
        picks[peer * keys : (peer + 1) * keys] = jnp.where(column == aim, 1.0, 0.0).astype(bf)

    heads.wait()
    tails.wait()

    def edge(buffer, chan, run):
        if run < 0 or run >= srcs:
            return jnp.zeros((HALO, src_rows), f32)
        tile = buffer[chan, run // 2 * 16 : run // 2 * 16 + 16].astype(f32)
        return tile[run % 2 * HALO : run % 2 * HALO + HALO]

    for chan in range(2):
        for run in range(srcs):
            below = jnp.where(last_rcv, edge(head_rx, chan, run + 1), edge(head_rx, chan, run))
            above = jnp.where(first_rcv, edge(tail_rx, chan, run - 1), edge(tail_rx, chan, run))
            rim = jnp.concatenate([below, above], axis=0).astype(bf)
            rims[chan, run] = rim
            main = slice(run * run_len, (run + 1) * run_len)
            first_tx[chan, run, :run_len] = rec[chan, main, :128]
            first_tx[chan, run, run_len:] = rim[:, :128]
            last_tx[chan, run, :run_len] = rec[chan, main, src_rows - 128 :]
            last_tx[chan, run, run_len:] = rim[:, src_rows - 128 :]

    low = jnp.maximum(src - 1, 0)
    high = jnp.minimum(src + 1, srcs - 1)
    firsts = remote(first_tx, after_rx, edge_send.at[2], edge_recv.at[2], (low, rcv))
    lasts = remote(last_tx, before_rx, edge_send.at[3], edge_recv.at[3], (high, rcv))

    @pl.when(src > 0)
    def _():
        firsts.start()

    @pl.when(src < srcs - 1)
    def _():
        lasts.start()

    def line(owner_spot, source, up, step, chan):
        owner = 2 * owner_spot + core
        shift = 2 if up else -2
        return remote(
            source, shard(owner, chan), line_send.at[chan, 0 if up else 1, step],
            left_recv.at[chan, owner], (src, jnp.clip(rcv + shift, 0, rcvs - 1)),
        )

    def hand(owner, source, chan):
        return remote(
            source, shard(owner, chan), pair_send.at[chan, owner // 2], left_recv.at[chan, owner],
            (src, rcv + 1 - 2 * core),
        )

    def shard(owner, chan):
        return left.at[
            pl.ds(pl.multiple_of(owner * run_len, 16), run_len), pl.ds(chan * panel, panel)
        ]

    to_prev, to_next = [], []
    for chan in range(2):
        for index, step in enumerate(range(1, rcvs)):
            peer = lax.rem(rcv + rcvs - step, rcvs)
            remote(
                front_tx.at[peer, chan], front_rx.at[peer, chan], front_send.at[chan, index],
                front_recv.at[chan, peer], (src, peer),
            ).wait_recv()
        for index, step in enumerate(range(1, srcs)):
            peer = lax.rem(src + srcs - step, srcs)
            remote(
                behind_tx.at[peer, chan], behind_rx.at[peer, chan], behind_send.at[chan, index],
                behind_recv.at[chan, peer], (peer, rcv),
            ).wait_recv()
        total = jnp.zeros((run_len, panel), f32)
        for peer in range(rcvs):
            total = total + jnp.dot(
                front_rx[peer, chan], picks[peer * keys : (peer + 1) * keys],
                preferred_element_type=f32,
            )
        for peer in range(srcs):
            shape = (rcvs * each, panel)
            index = lax.broadcasted_iota(jnp.int32, shape, 0)
            column = lax.broadcasted_iota(jnp.int32, shape, 1)
            pick = jnp.where(column == index + peer * rcvs * each, 1.0, 0.0).astype(bf)
            total = total + jnp.dot(behind_rx[peer, chan], pick, preferred_element_type=f32)
        own[chan, :run_len] = (total * 0.5).astype(bf)
        mine = own.at[chan, pl.ds(0, run_len)]

        @pl.when(spot < spots - 1)
        def _():
            line(spot, mine, True, 0, chan).start()

        @pl.when(spot > 0)
        def _():
            line(spot, mine, False, 0, chan).start()

        hand(rcv, mine, chan).start()
        to_prev.append(
            remote(
                own.at[chan, pl.ds(0, 16)], next_rx.at[chan], edge_send.at[4 + chan],
                edge_recv.at[4 + chan], prev_dev,
            )
        )
        to_next.append(
            remote(
                own.at[chan, pl.ds(run_len - 16, 16)], prev_rx.at[chan], edge_send.at[6 + chan],
                edge_recv.at[6 + chan], next_dev,
            )
        )

        @pl.when(has_prev)
        def _():
            to_prev[chan].start()

        @pl.when(has_next)
        def _():
            to_next[chan].start()

        left[
            pl.ds(pl.multiple_of(rcv * run_len, 16), run_len), chan * panel : (chan + 1) * panel
        ] = own[chan, :run_len]

    @pl.when(has_next)
    def _():
        for chan in range(2):
            to_prev[chan].wait_recv()

    @pl.when(jnp.logical_not(has_next))
    def _():
        next_rx[...] = jnp.zeros_like(next_rx)

    @pl.when(has_prev)
    def _():
        for chan in range(2):
            to_next[chan].wait_recv()

    @pl.when(jnp.logical_not(has_prev))
    def _():
        prev_rx[...] = jnp.zeros_like(prev_rx)

    place = lax.broadcasted_iota(jnp.int32, (2, 2 * HALO, panel), 1)
    own[:, run_len:] = jnp.where(place < HALO, next_rx[...], prev_rx[...])
    rights = []
    for index, peer in enumerate(src_peers):
        copy = remote(own, right.at[src], right_send.at[index], right_recv.at[src], (peer, rcv))
        copy.start()
        rights.append(copy)
    right[src] = own[...]

    def rim_copy(start, chan, index, which, peer):
        return remote(
            own.at[chan, pl.ds(run_len, 2 * HALO)],
            left.at[pl.ds(start, 2 * HALO), pl.ds(chan * panel, panel)],
            rim_send.at[chan, index], rim_recv.at[chan, which], (src, peer),
        )

    rim_ends = ((first_rcv, width - 2 * HALO, 0), (last_rcv, src_rows, 1))
    for holds, start, which in rim_ends:

        @pl.when(holds)
        def _():
            for chan in range(2):
                for index, peer in enumerate(rcv_peers):
                    rim_copy(start, chan, index, which, peer).start()
                left[start : start + 2 * HALO, chan * panel : (chan + 1) * panel] = own[
                    chan, run_len:
                ]

    def set_right(run):
        real, imag = right[run, 0], right[run, 1]
        top = slice(run * rows, (run + 1) * rows)
        bottom = slice((srcs + run) * rows, (srcs + run + 1) * rows)
        right_all[top, :panel] = real
        right_all[top, panel:] = -imag
        right_all[bottom, :panel] = imag
        right_all[bottom, panel:] = real

    def multiply(start, size):
        at = pl.ds(start, size)
        tiles[:, :, :, at] = lax.dot_general(
            right_all[...], left[at, :], (((1,), (1,)), ((), ())), preferred_element_type=f32
        ).reshape(2, srcs, rows, size)

    def out_copy(start, size, index):
        return pltpu.make_async_copy(
            tiles.at[:, :, :, pl.ds(start, size)],
            pred.at[:, :, :, pl.ds(start, size)],
            out_sem.at[index],
        )

    span = 2 * run_len

    def tile_of(owner_spot):
        for chan in range(2):
            hand(2 * owner_spot + 1 - core, shard(rcv, chan), chan).wait_recv()
        start = pl.multiple_of(owner_spot * span, 128)
        multiply(start, span)
        out_copy(start, span, owner_spot).start()

    def tiles_when(ready):
        @pl.loop(0, spots)
        def _(other):
            @pl.when(ready(jnp.abs(other - spot)))
            def _():
                tile_of(other)

    for step in range(1, spots):
        if step == spots - 1:
            for other in range(1, srcs):
                peer = lax.rem(src + srcs - other, srcs)
                remote(
                    own, right.at[peer], right_send.at[0], right_recv.at[peer], (peer, rcv)
                ).wait_recv()
            for run in range(srcs):
                set_right(run)
            tiles_when(lambda gap: gap < spots - 1)
        for chan in range(2):
            for up in (True, False):
                owner_spot = spot - step if up else spot + step
                arrives = spot >= step if up else spot + step < spots
                onward = spot < spots - 1 if up else spot > 0

                @pl.when(arrives)
                def _():
                    owner = 2 * owner_spot + core
                    block = shard(owner, chan)
                    line(owner_spot, block, up, step - 1, chan).wait_recv()
                    if step < spots - 1:

                        @pl.when(onward)
                        def _():
                            line(owner_spot, block, up, step, chan).start()

                    hand(owner, block, chan).start()

    for holds, start, which in rim_ends:

        @pl.when(jnp.logical_not(holds))
        def _():
            for chan in range(2):
                rim_copy(start, chan, 0, which, rcv).wait_recv()

    multiply(src_rows, 128)
    out_copy(src_rows, 128, spots).start()
    tiles_when(lambda gap: gap == spots - 1)

    for copy in fronts + behinds:
        copy.wait_send()

    @pl.when(src > 0)
    def _():
        firsts.wait_send()
        lasts.wait_recv()

    @pl.when(src < srcs - 1)
    def _():
        lasts.wait_send()
        firsts.wait_recv()

    @pl.when(src == 0)
    def _():
        before_rx[...] = jnp.zeros_like(before_rx)

    @pl.when(src == srcs - 1)
    def _():
        after_rx[...] = jnp.zeros_like(after_rx)

    lane = lax.broadcasted_iota(jnp.int32, (rows, 128), 1)
    zero = jnp.zeros((rows, 128), bf)
    for chan in range(2):
        for run in range(srcs):
            sides[chan, run] = jnp.where(
                lane < HALO, after_rx[chan, run], jnp.where(lane >= 128 - HALO, before_rx[chan, run], zero)
            )

    for chan in range(2):

        @pl.when(has_prev)
        def _():
            to_prev[chan].wait_send()

        @pl.when(has_next)
        def _():
            to_next[chan].wait_send()

        for holds, start, which in rim_ends:

            @pl.when(holds)
            def _():
                for index, peer in enumerate(rcv_peers):
                    rim_copy(start, chan, index, which, peer).wait_send()

        mine = own.at[chan, pl.ds(0, run_len)]
        for step in range(spots - 1):

            @pl.when(jnp.logical_and(spot < spots - 1, spot >= step))
            def _():
                line(spot, mine, True, step, chan).wait_send()

            @pl.when(jnp.logical_and(spot > 0, spot + step < spots))
            def _():
                line(spot, mine, False, step, chan).wait_send()

        for index in range(spots):
            hand(2 * index + core, mine, chan).wait_send()

    for copy in rights:
        copy.wait_send()
    for index in range(spots):
        out_copy(index * span, span, index).wait()
    out_copy(src_rows, 128, spots).wait()


def exchange_call(rec, panel_offset, srcs, rcvs):
    _, rcv_cols, src_rows = rec.shape
    run_len = rcv_cols // srcs
    rows = run_len + 2 * HALO
    panel = panel_offset.shape[0]
    each = panel // (srcs * rcvs)
    bf = jnp.bfloat16
    vmem = pl.BlockSpec(memory_space=pltpu.VMEM)
    front = (rcvs, 2, run_len, srcs * each)
    behind = (srcs, 2, run_len, rcvs * each)
    edges = (2, HALO * srcs, src_rows)
    side = (2, srcs, rows, 128)
    shapes = [front, front, behind, behind, edges, edges, edges, edges, side, side, side, side]
    shapes += [(2, rows, panel), (2, 16, panel), (2, 16, panel), (panel, panel)]
    shapes += [(src_rows + 128, 2 * panel), (srcs, 2, rows, panel), (2 * srcs * rows, 2 * panel)]
    wide = (2, srcs, rows, src_rows + 128)
    dma = pltpu.SemaphoreType.DMA
    return pl.pallas_call(
        functools.partial(exchange_kernel, (srcs, rcvs)),
        out_shape=(
            jax.ShapeDtypeStruct(wide, jnp.float32),
            jax.ShapeDtypeStruct((2, srcs, 2 * HALO, src_rows), bf),
            jax.ShapeDtypeStruct(side, bf),
        ),
        in_specs=[vmem] * 2,
        out_specs=(pl.BlockSpec(memory_space=pl.ANY), vmem, vmem),
        scratch_shapes=[pltpu.VMEM(shape, bf) for shape in shapes]
        + [
            pltpu.VMEM(wide, jnp.float32),
            pltpu.VMEM((rcv_cols, srcs * each), bf),
            pltpu.VMEM((src_rows, rcvs * each), bf),
        ]
        + [
            dma((2, rcvs)), dma((2, rcvs)), dma((2, srcs)), dma((2, srcs)), dma((8,)), dma((8,)),
            dma((srcs,)), dma((srcs,)), dma((2, 2, rcvs // 2)), dma((2, rcvs)), dma((2, rcvs // 2)),
            dma((2, rcvs)), dma((2, 2)), dma((rcvs // 2 + 1,)),
        ],
        compiler_params=pltpu.CompilerParams(
            collective_id=0, has_side_effects=True, vmem_limit_bytes=56 * 1024 * 1024
        ),
        cost_estimate=pl.CostEstimate(
            flops=10_000_000_000, bytes_accessed=8 * rec.size, transcendentals=0
        ),
    )(rec, panel_offset.reshape(1, panel))


def shards(record, panel_offset):
    src_count = lax.axis_size("src")
    rcv_count = lax.axis_size("rcv")
    freqs, _, rcv_cols, src_rows = record.shape
    run_len = rcv_cols // src_count
    if freqs != 1 or run_len % 16 or src_rows % 128 or src_count % 2 or rcv_count % 2 or run_len % 64 or rcv_count < 4:
        return plain_shards(record, panel_offset)
    pred, rims, sides = exchange_call(record[0], panel_offset, src_count, rcv_count)
    return sweep_call(record, rims, sides, pred, panel_offset.shape[0])


def solution(mesh):
    in_specs = (P(None, None, "rcv", "src"), P())
    out_specs = (P(None, None, "rcv", "src"), P(None, None, "rcv", "src"))
    return jax.shard_map(shards, mesh=mesh, in_specs=in_specs, out_specs=out_specs, check_vma=False)
```

```python
import functools

import jax
import jax.numpy as jnp
from jax import lax
from jax.experimental import pallas as pl
from jax.experimental.pallas import tpu as pltpu
from jax.sharding import PartitionSpec as P

STRIDE = 8
REACH = 4
SWEEPS = 2


weight_eps = 1e-06


def extended(cells, sides, width, closed):
    for axis, dim in sides:
        count = lax.axis_size(axis)
        ends = count if closed else count - 1
        head = lax.slice_in_dim(cells, 0, width, axis=dim)
        tail = lax.slice_in_dim(cells, cells.shape[dim] - width, cells.shape[dim], axis=dim)
        cells = jnp.concatenate(
            [
                lax.ppermute(tail, axis, [(i, (i + 1) % count) for i in range(ends)]),
                cells,
                lax.ppermute(head, axis, [((i + 1) % count, i) for i in range(ends)]),
            ],
            axis=dim,
        )
    return cells


def reorder_keys(values, rcv_count, src_count):
    full_shape = values.shape
    grouped = values.reshape(
        full_shape[:-1] + (rcv_count, src_count, full_shape[-1] // (rcv_count * src_count))
    )
    return jnp.swapaxes(grouped, -3, -2).reshape(full_shape)


def average_pair(first_part, second_part):
    return ((first_part.astype(jnp.float32) + second_part.astype(jnp.float32)) * 0.5).astype(
        jnp.bfloat16
    )


def cross_dot(left_mat, right_mat):
    return lax.dot_general(
        left_mat, right_mat, (((2,), (2,)), ((0,), (0,))), preferred_element_type=jnp.float32
    )


def predict_block(right_side, left_side):
    right_real = right_side[:, 0]
    right_imag = right_side[:, 1]
    left_real = left_side[:, 0]
    left_imag = left_side[:, 1]
    pred_real = cross_dot(right_real, left_real) - cross_dot(right_imag, left_imag)
    pred_imag = cross_dot(right_real, left_imag) + cross_dot(right_imag, left_real)
    return jnp.stack([pred_real, pred_imag], axis=1)


def neighbour_sum(partial_terms, src_count, rcv_pos, rcv_count):
    freq_count, chan_count, rcv_cols, src_rows = partial_terms.shape
    run_len = rcv_cols // src_count
    runs_view = partial_terms.reshape(freq_count, chan_count, src_count, run_len, src_rows)
    padded = extended(runs_view.astype(jnp.bfloat16), (("rcv", 3),), REACH, True).astype(
        runs_view.dtype
    )
    lower_rim = padded[:, :, :, :REACH]
    middle = padded[:, :, :, REACH : REACH + run_len]
    upper_rim = padded[:, :, :, REACH + run_len :]
    zero_rim = jnp.zeros_like(lower_rim[:, :, :1])
    lower_rim = jnp.where(
        rcv_pos == 0, jnp.concatenate([zero_rim, lower_rim[:, :, :-1]], axis=2), lower_rim
    )
    upper_rim = jnp.where(
        rcv_pos == rcv_count - 1,
        jnp.concatenate([upper_rim[:, :, 1:], zero_rim], axis=2),
        upper_rim,
    )
    padded = jnp.concatenate([lower_rim, middle, upper_rim], axis=3)
    recv_total = padded[:, :, :, 0:run_len]
    for shift_pos in range(1, 2 * REACH + 1):
        recv_total = recv_total + padded[:, :, :, shift_pos : shift_pos + run_len]
    recv_total = recv_total.reshape(freq_count, chan_count, rcv_cols, src_rows)
    src_padded = extended(recv_total.astype(jnp.bfloat16), (("src", 3),), REACH, False).astype(
        recv_total.dtype
    )
    box_totals = src_padded[..., 0:src_rows]
    for shift_pos in range(1, 2 * REACH + 1):
        box_totals = box_totals + src_padded[..., shift_pos : shift_pos + src_rows]
    return box_totals


def run_sweeps(data_bf, pred_bf, summer):
    data_f32 = data_bf.astype(jnp.float32)
    pred_f32 = pred_bf.astype(jnp.float32)
    data_real = data_f32[:, 0]
    data_imag = data_f32[:, 1]
    pred_real = pred_f32[:, 0]
    pred_imag = pred_f32[:, 1]
    err_real = data_real
    err_imag = data_imag
    for sweep_step in range(SWEEPS):
        weight = 1.5 - jnp.tanh(err_real * err_real + err_imag * err_imag)
        partial_terms = jnp.stack(
            [
                weight * (pred_real * data_real + pred_imag * data_imag),
                weight * (pred_real * data_imag - pred_imag * data_real),
                weight * (pred_real * pred_real + pred_imag * pred_imag),
            ],
            axis=1,
        )
        box_totals = summer(partial_terms)
        denom = box_totals[:, 2] + weight_eps
        gain_real = box_totals[:, 0] / denom
        gain_imag = box_totals[:, 1] / denom
        err_real = data_real - (gain_real * pred_real - gain_imag * pred_imag)
        err_imag = data_imag - (gain_real * pred_imag + gain_imag * pred_real)
    return jnp.stack([err_real, err_imag], axis=1)


def plain_shards(record, panel_offset):
    src_count = lax.axis_size("src")
    rcv_count = lax.axis_size("rcv")
    src_pos = lax.axis_index("src")
    rcv_pos = lax.axis_index("rcv")
    rcv_cols = record.shape[2]
    src_rows = record.shape[3]
    run_len = rcv_cols // src_count
    per_run = run_len // STRIDE
    panel_len = panel_offset.shape[0]
    run_ids = jnp.arange(src_count, dtype=jnp.int32)[:, None]
    within = jnp.arange(per_run, dtype=jnp.int32)[None, :]
    col_groups = (src_rows * run_ids + run_len * rcv_pos) // STRIDE + within
    col_index = (run_len * run_ids + STRIDE * within + jnp.take(panel_offset, col_groups)).reshape(
        -1
    )
    row_groups = jnp.arange(src_rows // STRIDE, dtype=jnp.int32)
    row_index = STRIDE * row_groups + jnp.take(
        panel_offset, src_rows // STRIDE * src_pos + row_groups
    )
    col_piece = jnp.swapaxes(jnp.take(record, col_index, axis=2), 2, 3)
    row_piece = jnp.take(record, row_index, axis=3)
    own_front = reorder_keys(
        lax.all_to_all(col_piece, "rcv", split_axis=2, concat_axis=3, tiled=True),
        rcv_count,
        src_count,
    )
    own_behind = lax.all_to_all(row_piece, "src", split_axis=2, concat_axis=3, tiled=True)
    owned_rows = average_pair(own_front, own_behind)
    right_side = lax.all_gather(owned_rows, "src", axis=2, tiled=True)
    prediction = predict_block(right_side, lax.all_gather(owned_rows, "rcv", axis=2, tiled=True))
    pred_round = lax.optimization_barrier(prediction.astype(jnp.bfloat16))
    multiples = (prediction * panel_len ** (-0.5)).astype(jnp.bfloat16)

    def runs_total(partial_terms):
        return neighbour_sum(partial_terms, src_count, rcv_pos, rcv_count)

    primaries = run_sweeps(record, pred_round, runs_total).astype(jnp.bfloat16)
    return (primaries, multiples)

HALO = 2 * REACH
MESH = pl.DeviceIdType.MESH


def wide_spans(width):
    spans = [(start, 256) for start in range(0, width - 255, 256)]
    done = 256 * (width // 256)
    return spans + ([(done, width - done)] if done < width else [])


def band(shape, shift, period):
    rows = lax.broadcasted_iota(jnp.int32, shape, 0)
    cols = lax.broadcasted_iota(jnp.int32, shape, 1) + shift
    gap = jnp.abs(rows - cols)
    if period:
        gap = jnp.minimum(gap, period - gap)
    return jnp.where(gap <= REACH, 1.0, 0.0).astype(jnp.bfloat16)


def sweep_kernel(
    scale, record_ref, rim_ref, side_ref, pred_ref, prim_ref, mult_ref,
    data, predb, terms, partial, totals, row_band, lane_band
):
    runs_len = record_ref.shape[2]
    src_rows = record_ref.shape[3]
    rows = runs_len + 2 * HALO
    width = src_rows + 128
    f32, bf = jnp.float32, jnp.bfloat16

    @pl.when(pl.program_id(0) == 0)
    def _():
        row_band[...] = band((rows, rows), 0, rows)
        lane_band[...] = band((512, 256), 128, 0)

    for chan in range(2):
        data[chan, :runs_len, :src_rows] = record_ref[0, chan]
        data[chan, runs_len:, :src_rows] = rim_ref[chan, 0]
        data[chan, :, src_rows:] = side_ref[chan, 0]

    def put_terms(at, lanes, err, here, guess):
        weight = 1.5 - jnp.tanh(err[0] * err[0] + err[1] * err[1])
        parts = (
            guess[0] * here[0] + guess[1] * here[1],
            guess[0] * here[1] - guess[1] * here[0],
            guess[0] * guess[0] + guess[1] * guess[1],
        )
        for index, part in enumerate(parts):
            terms[index, at, lanes] = (weight * part).astype(bf)

    def new_err(at, lanes):
        here = [data[chan, at, lanes].astype(f32) for chan in range(2)]
        guess = [predb[chan, at, lanes].astype(f32) for chan in range(2)]
        inverse = 1.0 / (totals[2, at, lanes] + weight_eps)
        gain_real = totals[0, at, lanes] * inverse
        gain_imag = totals[1, at, lanes] * inverse
        err = (
            here[0] - (gain_real * guess[0] - gain_imag * guess[1]),
            here[1] - (gain_real * guess[1] + gain_imag * guess[0]),
        )
        return err, here, guess

    def box():
        for index in range(3):
            for start, size in wide_spans(width):
                partial[index, :, 128 + start : 128 + start + size] = jnp.dot(
                    row_band[...], terms[index, :, start : start + size], preferred_element_type=f32
                ).astype(bf)
            partial[index, :, :128] = partial[index, :, width : width + 128]
            partial[index, :, width + 128 :] = partial[index, :, 128:256]
        for index in range(3):
            for start, size in wide_spans(width):
                totals[index, :, start : start + size] = jnp.dot(
                    partial[index, :, start : start + size + 256],
                    lane_band[: size + 256, :size],
                    preferred_element_type=f32,
                )

    @pl.loop(0, rows // 16)
    def _(step):
        at = pl.ds(pl.multiple_of(step * 16, 16), 16)
        for block in range(width // 128):
            lanes = slice(block * 128, (block + 1) * 128)
            here = [data[chan, at, lanes].astype(f32) for chan in range(2)]
            guess = []
            for chan in range(2):
                rounded = pred_ref[chan, 0, at, lanes].astype(bf)
                predb[chan, at, lanes] = rounded
                guess.append(rounded.astype(f32))
            put_terms(at, lanes, here, here, guess)

    @pl.loop(0, runs_len // 16)
    def _(step):
        at = pl.ds(pl.multiple_of(step * 16, 16), 16)
        for block in range(src_rows // 128):
            lanes = slice(block * 128, (block + 1) * 128)
            for chan in range(2):
                mult_ref[0, chan, at, lanes] = (pred_ref[chan, 0, at, lanes] * scale).astype(bf)

    for sweep_step in range(SWEEPS - 1):
        box()

        @pl.loop(0, rows // 16)
        def _(step):
            at = pl.ds(pl.multiple_of(step * 16, 16), 16)
            for block in range(width // 128):
                lanes = slice(block * 128, (block + 1) * 128)
                put_terms(at, lanes, *new_err(at, lanes))

    box()

    @pl.loop(0, runs_len // 16)
    def _(step):
        at = pl.ds(pl.multiple_of(step * 16, 16), 16)
        for block in range(src_rows // 128):
            lanes = slice(block * 128, (block + 1) * 128)
            err, _, _ = new_err(at, lanes)
            prim_ref[0, 0, at, lanes] = err[0].astype(bf)
            prim_ref[0, 1, at, lanes] = err[1].astype(bf)


def sweep_call(record, rims, sides, pred, panel):
    _, _, rcv_cols, src_rows = record.shape
    _, runs, rows, width = pred.shape
    run_len = rcv_cols // runs
    f32, bf = jnp.float32, jnp.bfloat16
    out = jax.ShapeDtypeStruct(record.shape, bf)
    tile = pl.BlockSpec((1, 2, run_len, src_rows), lambda r: (0, 0, r, 0))
    return pl.pallas_call(
        functools.partial(sweep_kernel, panel ** (-0.5)),
        grid=(runs,),
        out_shape=(out, out),
        in_specs=[
            tile,
            pl.BlockSpec((2, 1, 2 * HALO, src_rows), lambda r: (0, r, 0, 0)),
            pl.BlockSpec((2, 1, rows, 128), lambda r: (0, r, 0, 0)),
            pl.BlockSpec((2, 1, rows, width), lambda r: (0, r, 0, 0)),
        ],
        out_specs=(tile, tile),
        scratch_shapes=[
            pltpu.VMEM((2, rows, width), bf),
            pltpu.VMEM((2, rows, width), bf),
            pltpu.VMEM((3, rows, width), bf),
            pltpu.VMEM((3, rows, width + 256), bf),
            pltpu.VMEM((3, rows, width), f32),
            pltpu.VMEM((rows, rows), bf),
            pltpu.VMEM((512, 256), bf),
        ],
        compiler_params=pltpu.CompilerParams(vmem_limit_bytes=56 * 1024 * 1024),
        cost_estimate=pl.CostEstimate(
            flops=12_000_000_000, bytes_accessed=4 * record.size * 2, transcendentals=2 * record.size
        ),
    )(record, rims, sides, pred)


def roll(values, shift):
    return pltpu.roll(values, shift % 128, 1) if shift % 128 else values


def lanes_of(values):
    return lax.broadcasted_iota(jnp.int32, values.shape, 1)


def pack_traces(traces):
    half, quarter = traces.shape[0] // 2, traces.shape[0] // 4
    wide = jnp.where(
        lanes_of(traces[:half]) < 64, traces[:half], roll(traces[half:], 64)
    )
    lane = lanes_of(traces[:quarter])
    rest = jnp.zeros((quarter, 128), traces.dtype)
    for part in range(4):
        moved = roll(traces[part * quarter : (part + 1) * quarter], 32 * part - 64)
        rest = jnp.where(lane // 32 == part, moved, rest)
    return jnp.concatenate([wide, rest], axis=0)


def unpack_traces(packed):
    half = packed.shape[0] * 2 // 3
    wide = jnp.concatenate([packed[:half], roll(packed[:half], 64)], axis=0)
    rest = jnp.concatenate([roll(packed[half:], 64 - 32 * part) for part in range(4)], axis=0)
    lane = lanes_of(wide)
    return jnp.where(lane < 64, wide, jnp.where(lane < 96, rest, jnp.zeros_like(rest)))


def exchange_kernel(
    sizes, rec, offset, pred, rims, sides,
    front_tx, front_rx, behind_tx, behind_rx, head_tx, head_rx, tail_tx, tail_rx,
    first_tx, after_rx, last_tx, before_rx, own, next_rx, prev_rx, picks, left, right, right_all, tiles,
    col_pick, row_pick, gathered,
    front_send, front_recv, behind_send, behind_recv, edge_send, edge_recv,
    right_send, right_recv, line_send, left_recv, pair_send, rim_send, rim_recv, out_sem,
):
    srcs, rcvs = sizes
    src = lax.axis_index("src")
    rcv = lax.axis_index("rcv")
    f32, bf = jnp.float32, jnp.bfloat16
    rcv_cols, src_rows = rec.shape[1:]
    run_len = rcv_cols // srcs
    rows = run_len + 2 * HALO
    width = src_rows + 128
    panel = right.shape[3]
    each = panel // (srcs * rcvs)
    spots = rcvs // 2
    spot, core = rcv // 2, lax.rem(rcv, 2)

    def remote(source, target, send, recv, where):
        return pltpu.make_async_remote_copy(
            src_ref=source, dst_ref=target, send_sem=send, recv_sem=recv,
            device_id=where, device_id_type=MESH,
        )

    rcv_peers = [lax.rem(rcv + step, rcvs) for step in range(1, rcvs)]
    src_peers = [lax.rem(src + step, srcs) for step in range(1, srcs)]
    last_rcv, first_rcv = rcv == rcvs - 1, rcv == 0
    has_next = jnp.logical_not(jnp.logical_and(last_rcv, src == srcs - 1))
    has_prev = jnp.logical_not(jnp.logical_and(first_rcv, src == 0))
    next_dev = (
        jnp.where(last_rcv, jnp.minimum(src + 1, srcs - 1), src), jnp.where(last_rcv, 0, rcv + 1)
    )
    prev_dev = (
        jnp.where(first_rcv, jnp.maximum(src - 1, 0), src), jnp.where(first_rcv, rcvs - 1, rcv - 1)
    )
    far_next = jnp.logical_and(last_rcv, src < srcs - 1)
    far_prev = jnp.logical_and(first_rcv, src > 0)

    left[src_rows:] = jnp.zeros((128, 2 * panel), bf)
    barrier = pltpu.get_barrier_semaphore()
    for peer in rcv_peers:
        pl.semaphore_signal(barrier, inc=1, device_id=(src, peer), device_id_type=MESH)
    for peer in src_peers:
        pl.semaphore_signal(barrier, inc=1, device_id=(peer, rcv), device_id_type=MESH)

    @pl.when(far_next)
    def _():
        pl.semaphore_signal(barrier, inc=1, device_id=next_dev, device_id_type=MESH)

    @pl.when(far_prev)
    def _():
        pl.semaphore_signal(barrier, inc=1, device_id=prev_dev, device_id_type=MESH)

    offsets = jnp.broadcast_to(offset[...].astype(f32), (8, panel)).astype(bf)

    def pick_from(target, count, group_of, cell_of):
        groups = lax.broadcasted_iota(jnp.int32, (panel, count), 0)
        column = lax.broadcasted_iota(jnp.int32, (panel, count), 1)
        chosen = jnp.where(groups == group_of(column), 1.0, 0.0).astype(bf)
        mine = jnp.dot(offsets, chosen, preferred_element_type=f32)[:1].astype(jnp.int32)
        cells = lax.broadcasted_iota(jnp.int32, target.shape, 0)
        column = lax.broadcasted_iota(jnp.int32, (1, count), 1)
        target[...] = jnp.where(cells == cell_of(column) + mine, 1.0, 0.0).astype(bf)

    per_src = rcvs * each
    key = lax.broadcasted_iota(jnp.int32, (128, panel), 0)
    groups = lax.broadcasted_iota(jnp.int32, (128, panel), 1)
    chosen = jnp.where(
        groups == key // each * per_src + each * rcv + key % each, 1.0, 0.0
    ).astype(bf)
    mine = lax.dot_general(
        chosen, offsets, (((1,), (1,)), ((), ())), preferred_element_type=f32
    )[:, :1].astype(jnp.int32)
    cells = lax.broadcasted_iota(jnp.int32, (128, rcv_cols), 1)
    key = lax.broadcasted_iota(jnp.int32, (128, 1), 0)
    cell = key // each * run_len + STRIDE * (key % each) + mine
    cell = jnp.where(key < srcs * each, cell, -1)
    col_pick[...] = jnp.where(cells == cell, 1.0, 0.0).astype(bf)
    pick_from(row_pick, per_src, lambda j: per_src * src + j, lambda j: STRIDE * j)

    for chan in range(2):
        for pair in range(srcs // 2):
            for buffer, start in ((head_tx, 0), (tail_tx, run_len - 16)):
                ends = [
                    rec[chan, run * run_len + start : run * run_len + start + 16].astype(f32)
                    for run in (2 * pair, 2 * pair + 1)
                ]
                part = slice(0, HALO) if start == 0 else slice(16 - HALO, 16)
                buffer[chan, 16 * pair : 16 * pair + 16] = jnp.concatenate(
                    [end[part] for end in ends], axis=0
                ).astype(bf)

    pl.semaphore_wait(
        barrier,
        rcvs - 1 + srcs - 1 + jnp.where(far_next, 1, 0) + jnp.where(far_prev, 1, 0),
    )
    heads = remote(
        head_tx, head_rx, edge_send.at[0], edge_recv.at[0], (src, lax.rem(rcv + rcvs - 1, rcvs))
    )
    tails = remote(tail_tx, tail_rx, edge_send.at[1], edge_recv.at[1], (src, lax.rem(rcv + 1, rcvs)))
    heads.start()
    tails.start()

    fronts, behinds = [], []
    for chan in range(2):
        picked = jnp.transpose(jnp.dot(col_pick[...], rec[chan], preferred_element_type=f32))
        for peer in range(rcvs):
            front_tx[peer, chan] = pack_traces(
                picked[peer * run_len : (peer + 1) * run_len]
            ).astype(bf)
        for index, peer in enumerate(rcv_peers):
            copy = remote(
                front_tx.at[peer, chan], front_rx.at[rcv, chan], front_send.at[chan, index],
                front_recv.at[chan, rcv], (src, peer),
            )
            copy.start()
            fronts.append(copy)
        front_rx[rcv, chan] = front_tx[rcv, chan]
    for chan in range(2):
        picked = jnp.dot(rec[chan], row_pick[...], preferred_element_type=f32).astype(bf)
        for peer in range(srcs):
            behind_tx[peer, chan] = picked[peer * run_len : (peer + 1) * run_len]
        for index, peer in enumerate(src_peers):
            copy = remote(
                behind_tx.at[peer, chan], behind_rx.at[src, chan], behind_send.at[chan, index],
                behind_recv.at[chan, src], (peer, rcv),
            )
            copy.start()
            behinds.append(copy)
        behind_rx[src, chan] = behind_tx[src, chan]

    for peer in range(rcvs):
        index = lax.broadcasted_iota(jnp.int32, (128, panel), 0)
        column = lax.broadcasted_iota(jnp.int32, (128, panel), 1)
        aim = index // each * (rcvs * each) + peer * each + index % each
        picks[peer * 128 : (peer + 1) * 128] = jnp.where(column == aim, 1.0, 0.0).astype(bf)

    heads.wait()
    tails.wait()

    def edge(buffer, chan, run):
        if run < 0 or run >= srcs:
            return jnp.zeros((HALO, src_rows), f32)
        tile = buffer[chan, run // 2 * 16 : run // 2 * 16 + 16].astype(f32)
        return tile[run % 2 * HALO : run % 2 * HALO + HALO]

    packs = [jnp.zeros((rows, 128), f32), jnp.zeros((rows, 128), f32)]
    for chan in range(2):
        for run in range(srcs):
            below = jnp.where(last_rcv, edge(head_rx, chan, run + 1), edge(head_rx, chan, run))
            above = jnp.where(first_rcv, edge(tail_rx, chan, run - 1), edge(tail_rx, chan, run))
            rim = jnp.concatenate([below, above], axis=0).astype(bf)
            rims[chan, run] = rim
            main = slice(run * run_len, (run + 1) * run_len)
            slot = chan * srcs + run
            for block, lanes in enumerate((slice(0, 128), slice(src_rows - 128, src_rows))):
                side = jnp.concatenate(
                    [rec[chan, main, lanes].astype(f32), rim[:, lanes].astype(f32)], axis=0
                )
                moved = roll(side, HALO * slot + HALO * block)
                packs[block] = jnp.where(lanes_of(side) // HALO == slot, moved, packs[block])
    first_tx[...] = packs[0].astype(bf)
    last_tx[...] = packs[1].astype(bf)

    low = jnp.maximum(src - 1, 0)
    high = jnp.minimum(src + 1, srcs - 1)
    firsts = remote(first_tx, after_rx, edge_send.at[2], edge_recv.at[2], (low, rcv))
    lasts = remote(last_tx, before_rx, edge_send.at[3], edge_recv.at[3], (high, rcv))

    @pl.when(src > 0)
    def _():
        firsts.start()

    @pl.when(src < srcs - 1)
    def _():
        lasts.start()

    def line(owner_spot, source, up, step, chan):
        owner = 2 * owner_spot + core
        shift = 2 if up else -2
        return remote(
            source, shard(owner, chan), line_send.at[chan, 0 if up else 1, step],
            left_recv.at[chan, owner], (src, jnp.clip(rcv + shift, 0, rcvs - 1)),
        )

    def hand(owner, source, chan):
        return remote(
            source, shard(owner, chan), pair_send.at[chan, owner // 2], left_recv.at[chan, owner],
            (src, rcv + 1 - 2 * core),
        )

    def shard(owner, chan):
        return left.at[
            pl.ds(pl.multiple_of(owner * run_len, 16), run_len), pl.ds(chan * panel, panel)
        ]

    to_prev, to_next = [], []
    for chan in range(2):
        for index, step in enumerate(range(1, rcvs)):
            peer = lax.rem(rcv + rcvs - step, rcvs)
            remote(
                front_tx.at[peer, chan], front_rx.at[peer, chan], front_send.at[chan, index],
                front_recv.at[chan, peer], (src, peer),
            ).wait_recv()
        for index, step in enumerate(range(1, srcs)):
            peer = lax.rem(src + srcs - step, srcs)
            remote(
                behind_tx.at[peer, chan], behind_rx.at[peer, chan], behind_send.at[chan, index],
                behind_recv.at[chan, peer], (peer, rcv),
            ).wait_recv()
        for peer in range(rcvs):
            gathered[:, peer * 128 : (peer + 1) * 128] = unpack_traces(
                front_rx[peer, chan].astype(f32)
            ).astype(bf)
        total = jnp.dot(gathered[...], picks[...], preferred_element_type=f32)
        for peer in range(srcs):
            shape = (rcvs * each, panel)
            index = lax.broadcasted_iota(jnp.int32, shape, 0)
            column = lax.broadcasted_iota(jnp.int32, shape, 1)
            pick = jnp.where(column == index + peer * rcvs * each, 1.0, 0.0).astype(bf)
            total = total + jnp.dot(behind_rx[peer, chan], pick, preferred_element_type=f32)
        own[chan, :run_len] = (total * 0.5).astype(bf)
        mine = own.at[chan, pl.ds(0, run_len)]

        @pl.when(spot < spots - 1)
        def _():
            line(spot, mine, True, 0, chan).start()

        @pl.when(spot > 0)
        def _():
            line(spot, mine, False, 0, chan).start()

        hand(rcv, mine, chan).start()
        to_prev.append(
            remote(
                own.at[chan, pl.ds(0, 16)], next_rx.at[chan], edge_send.at[4 + chan],
                edge_recv.at[4 + chan], prev_dev,
            )
        )
        to_next.append(
            remote(
                own.at[chan, pl.ds(run_len - 16, 16)], prev_rx.at[chan], edge_send.at[6 + chan],
                edge_recv.at[6 + chan], next_dev,
            )
        )

        @pl.when(has_prev)
        def _():
            to_prev[chan].start()

        @pl.when(has_next)
        def _():
            to_next[chan].start()

        left[
            pl.ds(pl.multiple_of(rcv * run_len, 16), run_len), chan * panel : (chan + 1) * panel
        ] = own[chan, :run_len]

    @pl.when(has_next)
    def _():
        for chan in range(2):
            to_prev[chan].wait_recv()

    @pl.when(jnp.logical_not(has_next))
    def _():
        next_rx[...] = jnp.zeros_like(next_rx)

    @pl.when(has_prev)
    def _():
        for chan in range(2):
            to_next[chan].wait_recv()

    @pl.when(jnp.logical_not(has_prev))
    def _():
        prev_rx[...] = jnp.zeros_like(prev_rx)

    place = lax.broadcasted_iota(jnp.int32, (2, 2 * HALO, panel), 1)
    own[:, run_len:] = jnp.where(place < HALO, next_rx[...], prev_rx[...])
    rights = []
    for index, peer in enumerate(src_peers):
        copy = remote(own, right.at[src], right_send.at[index], right_recv.at[src], (peer, rcv))
        copy.start()
        rights.append(copy)
    right[src] = own[...]

    def rim_copy(start, chan, index, which, peer):
        return remote(
            own.at[chan, pl.ds(run_len, 2 * HALO)],
            left.at[pl.ds(start, 2 * HALO), pl.ds(chan * panel, panel)],
            rim_send.at[chan, index], rim_recv.at[chan, which], (src, peer),
        )

    rim_ends = ((first_rcv, width - 2 * HALO, 0), (last_rcv, src_rows, 1))
    for holds, start, which in rim_ends:

        @pl.when(holds)
        def _():
            for chan in range(2):
                for index, peer in enumerate(rcv_peers):
                    rim_copy(start, chan, index, which, peer).start()
                left[start : start + 2 * HALO, chan * panel : (chan + 1) * panel] = own[
                    chan, run_len:
                ]

    def set_right(run):
        real, imag = right[run, 0], right[run, 1]
        top = slice(run * rows, (run + 1) * rows)
        bottom = slice((srcs + run) * rows, (srcs + run + 1) * rows)
        right_all[top, :panel] = real
        right_all[top, panel:] = -imag
        right_all[bottom, :panel] = imag
        right_all[bottom, panel:] = real

    def multiply(start, size):
        at = pl.ds(start, size)
        tiles[:, :, :, at] = lax.dot_general(
            right_all[...], left[at, :], (((1,), (1,)), ((), ())), preferred_element_type=f32
        ).reshape(2, srcs, rows, size)

    def out_copy(start, size, index):
        return pltpu.make_async_copy(
            tiles.at[:, :, :, pl.ds(start, size)],
            pred.at[:, :, :, pl.ds(start, size)],
            out_sem.at[index],
        )

    span = 2 * run_len

    def tile_of(owner_spot):
        for chan in range(2):
            hand(2 * owner_spot + 1 - core, shard(rcv, chan), chan).wait_recv()
        start = pl.multiple_of(owner_spot * span, 128)
        multiply(start, span)
        out_copy(start, span, owner_spot).start()

    def tiles_when(ready):
        @pl.loop(0, spots)
        def _(other):
            @pl.when(ready(jnp.abs(other - spot)))
            def _():
                tile_of(other)

    for step in range(1, spots):
        if step == spots - 1:
            for other in range(1, srcs):
                peer = lax.rem(src + srcs - other, srcs)
                remote(
                    own, right.at[peer], right_send.at[0], right_recv.at[peer], (peer, rcv)
                ).wait_recv()
            for run in range(srcs):
                set_right(run)
            tiles_when(lambda gap: gap < spots - 1)
            for holds, start, which in rim_ends:

                @pl.when(jnp.logical_not(holds))
                def _():
                    for chan in range(2):
                        rim_copy(start, chan, 0, which, rcv).wait_recv()

            multiply(src_rows, 128)
            out_copy(src_rows, 128, spots).start()
        for chan in range(2):
            for up in (True, False):
                owner_spot = spot - step if up else spot + step
                arrives = spot >= step if up else spot + step < spots
                onward = spot < spots - 1 if up else spot > 0

                @pl.when(arrives)
                def _():
                    owner = 2 * owner_spot + core
                    block = shard(owner, chan)
                    line(owner_spot, block, up, step - 1, chan).wait_recv()
                    if step < spots - 1:

                        @pl.when(onward)
                        def _():
                            line(owner_spot, block, up, step, chan).start()

                    hand(owner, block, chan).start()

    tiles_when(lambda gap: gap == spots - 1)

    for copy in fronts + behinds:
        copy.wait_send()

    @pl.when(src > 0)
    def _():
        firsts.wait_send()
        lasts.wait_recv()

    @pl.when(src < srcs - 1)
    def _():
        lasts.wait_send()
        firsts.wait_recv()

    @pl.when(src == 0)
    def _():
        before_rx[...] = jnp.zeros_like(before_rx)

    @pl.when(src == srcs - 1)
    def _():
        after_rx[...] = jnp.zeros_like(after_rx)

    after, before = after_rx[...].astype(f32), before_rx[...].astype(f32)
    lane = lanes_of(after)
    zero = jnp.zeros((rows, 128), f32)
    for chan in range(2):
        for run in range(srcs):
            slot = chan * srcs + run
            high_side = jnp.where(lane >= 128 - HALO, roll(before, 128 - HALO - HALO * slot), zero)
            sides[chan, run] = jnp.where(
                lane < HALO, roll(after, -HALO * slot), high_side
            ).astype(bf)

    for chan in range(2):

        @pl.when(has_prev)
        def _():
            to_prev[chan].wait_send()

        @pl.when(has_next)
        def _():
            to_next[chan].wait_send()

        for holds, start, which in rim_ends:

            @pl.when(holds)
            def _():
                for index, peer in enumerate(rcv_peers):
                    rim_copy(start, chan, index, which, peer).wait_send()

        mine = own.at[chan, pl.ds(0, run_len)]
        for step in range(spots - 1):

            @pl.when(jnp.logical_and(spot < spots - 1, spot >= step))
            def _():
                line(spot, mine, True, step, chan).wait_send()

            @pl.when(jnp.logical_and(spot > 0, spot + step < spots))
            def _():
                line(spot, mine, False, step, chan).wait_send()

        for index in range(spots):
            hand(2 * index + core, mine, chan).wait_send()

    for copy in rights:
        copy.wait_send()
    for index in range(spots):
        out_copy(index * span, span, index).wait()
    out_copy(src_rows, 128, spots).wait()


def exchange_call(rec, panel_offset, srcs, rcvs):
    _, rcv_cols, src_rows = rec.shape
    run_len = rcv_cols // srcs
    rows = run_len + 2 * HALO
    panel = panel_offset.shape[0]
    each = panel // (srcs * rcvs)
    bf = jnp.bfloat16
    vmem = pl.BlockSpec(memory_space=pltpu.VMEM)
    front = (rcvs, 2, run_len * 3 // 4, 128)
    behind = (srcs, 2, run_len, rcvs * each)
    edges = (2, HALO * srcs, src_rows)
    side = (2, srcs, rows, 128)
    pack = (rows, 128)
    shapes = [front, front, behind, behind, edges, edges, edges, edges, pack, pack, pack, pack]
    shapes += [(2, rows, panel), (2, 16, panel), (2, 16, panel), (rcvs * 128, panel)]
    shapes += [(src_rows + 128, 2 * panel), (srcs, 2, rows, panel), (2 * srcs * rows, 2 * panel)]
    wide = (2, srcs, rows, src_rows + 128)
    dma = pltpu.SemaphoreType.DMA
    return pl.pallas_call(
        functools.partial(exchange_kernel, (srcs, rcvs)),
        out_shape=(
            jax.ShapeDtypeStruct(wide, jnp.float32),
            jax.ShapeDtypeStruct((2, srcs, 2 * HALO, src_rows), bf),
            jax.ShapeDtypeStruct(side, bf),
        ),
        in_specs=[vmem] * 2,
        out_specs=(pl.BlockSpec(memory_space=pl.ANY), vmem, vmem),
        scratch_shapes=[pltpu.VMEM(shape, bf) for shape in shapes]
        + [
            pltpu.VMEM(wide, jnp.float32),
            pltpu.VMEM((128, rcv_cols), bf),
            pltpu.VMEM((src_rows, rcvs * each), bf),
            pltpu.VMEM((run_len, rcvs * 128), bf),
        ]
        + [
            dma((2, rcvs)), dma((2, rcvs)), dma((2, srcs)), dma((2, srcs)), dma((8,)), dma((8,)),
            dma((srcs,)), dma((srcs,)), dma((2, 2, rcvs // 2)), dma((2, rcvs)), dma((2, rcvs // 2)),
            dma((2, rcvs)), dma((2, 2)), dma((rcvs // 2 + 1,)),
        ],
        compiler_params=pltpu.CompilerParams(
            collective_id=0, has_side_effects=True, vmem_limit_bytes=56 * 1024 * 1024
        ),
        cost_estimate=pl.CostEstimate(
            flops=10_000_000_000, bytes_accessed=8 * rec.size, transcendentals=0
        ),
    )(rec, panel_offset.reshape(1, panel))


def shards(record, panel_offset):
    src_count = lax.axis_size("src")
    rcv_count = lax.axis_size("rcv")
    freqs, _, rcv_cols, src_rows = record.shape
    run_len = rcv_cols // src_count
    if freqs != 1 or run_len % 16 or src_rows % 128 or src_count % 2 or rcv_count % 2 or run_len % 64 or rcv_count < 4 or src_count * run_len > 96 * STRIDE or src_count * HALO > 64:
        return plain_shards(record, panel_offset)
    pred, rims, sides = exchange_call(record[0], panel_offset, src_count, rcv_count)
    return sweep_call(record, rims, sides, pred, panel_offset.shape[0])


def solution(mesh):
    in_specs = (P(None, None, "rcv", "src"), P())
    out_specs = (P(None, None, "rcv", "src"), P(None, None, "rcv", "src"))
    return jax.shard_map(shards, mesh=mesh, in_specs=in_specs, out_specs=out_specs, check_vma=False)
```

```python
import functools

import jax
import jax.numpy as jnp
from jax import lax
from jax.experimental import pallas as pl
from jax.experimental.pallas import tpu as pltpu
from jax.sharding import PartitionSpec as P

STRIDE = 8
REACH = 4
SWEEPS = 2


weight_eps = 1e-06


def extended(cells, sides, width, closed):
    for axis, dim in sides:
        count = lax.axis_size(axis)
        ends = count if closed else count - 1
        head = lax.slice_in_dim(cells, 0, width, axis=dim)
        tail = lax.slice_in_dim(cells, cells.shape[dim] - width, cells.shape[dim], axis=dim)
        cells = jnp.concatenate(
            [
                lax.ppermute(tail, axis, [(i, (i + 1) % count) for i in range(ends)]),
                cells,
                lax.ppermute(head, axis, [((i + 1) % count, i) for i in range(ends)]),
            ],
            axis=dim,
        )
    return cells


def reorder_keys(values, rcv_count, src_count):
    full_shape = values.shape
    grouped = values.reshape(
        full_shape[:-1] + (rcv_count, src_count, full_shape[-1] // (rcv_count * src_count))
    )
    return jnp.swapaxes(grouped, -3, -2).reshape(full_shape)


def average_pair(first_part, second_part):
    return ((first_part.astype(jnp.float32) + second_part.astype(jnp.float32)) * 0.5).astype(
        jnp.bfloat16
    )


def cross_dot(left_mat, right_mat):
    return lax.dot_general(
        left_mat, right_mat, (((2,), (2,)), ((0,), (0,))), preferred_element_type=jnp.float32
    )


def predict_block(right_side, left_side):
    right_real = right_side[:, 0]
    right_imag = right_side[:, 1]
    left_real = left_side[:, 0]
    left_imag = left_side[:, 1]
    pred_real = cross_dot(right_real, left_real) - cross_dot(right_imag, left_imag)
    pred_imag = cross_dot(right_real, left_imag) + cross_dot(right_imag, left_real)
    return jnp.stack([pred_real, pred_imag], axis=1)


def neighbour_sum(partial_terms, src_count, rcv_pos, rcv_count):
    freq_count, chan_count, rcv_cols, src_rows = partial_terms.shape
    run_len = rcv_cols // src_count
    runs_view = partial_terms.reshape(freq_count, chan_count, src_count, run_len, src_rows)
    padded = extended(runs_view.astype(jnp.bfloat16), (("rcv", 3),), REACH, True).astype(
        runs_view.dtype
    )
    lower_rim = padded[:, :, :, :REACH]
    middle = padded[:, :, :, REACH : REACH + run_len]
    upper_rim = padded[:, :, :, REACH + run_len :]
    zero_rim = jnp.zeros_like(lower_rim[:, :, :1])
    lower_rim = jnp.where(
        rcv_pos == 0, jnp.concatenate([zero_rim, lower_rim[:, :, :-1]], axis=2), lower_rim
    )
    upper_rim = jnp.where(
        rcv_pos == rcv_count - 1,
        jnp.concatenate([upper_rim[:, :, 1:], zero_rim], axis=2),
        upper_rim,
    )
    padded = jnp.concatenate([lower_rim, middle, upper_rim], axis=3)
    recv_total = padded[:, :, :, 0:run_len]
    for shift_pos in range(1, 2 * REACH + 1):
        recv_total = recv_total + padded[:, :, :, shift_pos : shift_pos + run_len]
    recv_total = recv_total.reshape(freq_count, chan_count, rcv_cols, src_rows)
    src_padded = extended(recv_total.astype(jnp.bfloat16), (("src", 3),), REACH, False).astype(
        recv_total.dtype
    )
    box_totals = src_padded[..., 0:src_rows]
    for shift_pos in range(1, 2 * REACH + 1):
        box_totals = box_totals + src_padded[..., shift_pos : shift_pos + src_rows]
    return box_totals


def run_sweeps(data_bf, pred_bf, summer):
    data_f32 = data_bf.astype(jnp.float32)
    pred_f32 = pred_bf.astype(jnp.float32)
    data_real = data_f32[:, 0]
    data_imag = data_f32[:, 1]
    pred_real = pred_f32[:, 0]
    pred_imag = pred_f32[:, 1]
    err_real = data_real
    err_imag = data_imag
    for sweep_step in range(SWEEPS):
        weight = 1.5 - jnp.tanh(err_real * err_real + err_imag * err_imag)
        partial_terms = jnp.stack(
            [
                weight * (pred_real * data_real + pred_imag * data_imag),
                weight * (pred_real * data_imag - pred_imag * data_real),
                weight * (pred_real * pred_real + pred_imag * pred_imag),
            ],
            axis=1,
        )
        box_totals = summer(partial_terms)
        denom = box_totals[:, 2] + weight_eps
        gain_real = box_totals[:, 0] / denom
        gain_imag = box_totals[:, 1] / denom
        err_real = data_real - (gain_real * pred_real - gain_imag * pred_imag)
        err_imag = data_imag - (gain_real * pred_imag + gain_imag * pred_real)
    return jnp.stack([err_real, err_imag], axis=1)


def plain_shards(record, panel_offset):
    src_count = lax.axis_size("src")
    rcv_count = lax.axis_size("rcv")
    src_pos = lax.axis_index("src")
    rcv_pos = lax.axis_index("rcv")
    rcv_cols = record.shape[2]
    src_rows = record.shape[3]
    run_len = rcv_cols // src_count
    per_run = run_len // STRIDE
    panel_len = panel_offset.shape[0]
    run_ids = jnp.arange(src_count, dtype=jnp.int32)[:, None]
    within = jnp.arange(per_run, dtype=jnp.int32)[None, :]
    col_groups = (src_rows * run_ids + run_len * rcv_pos) // STRIDE + within
    col_index = (run_len * run_ids + STRIDE * within + jnp.take(panel_offset, col_groups)).reshape(
        -1
    )
    row_groups = jnp.arange(src_rows // STRIDE, dtype=jnp.int32)
    row_index = STRIDE * row_groups + jnp.take(
        panel_offset, src_rows // STRIDE * src_pos + row_groups
    )
    col_piece = jnp.swapaxes(jnp.take(record, col_index, axis=2), 2, 3)
    row_piece = jnp.take(record, row_index, axis=3)
    own_front = reorder_keys(
        lax.all_to_all(col_piece, "rcv", split_axis=2, concat_axis=3, tiled=True),
        rcv_count,
        src_count,
    )
    own_behind = lax.all_to_all(row_piece, "src", split_axis=2, concat_axis=3, tiled=True)
    owned_rows = average_pair(own_front, own_behind)
    right_side = lax.all_gather(owned_rows, "src", axis=2, tiled=True)
    prediction = predict_block(right_side, lax.all_gather(owned_rows, "rcv", axis=2, tiled=True))
    pred_round = lax.optimization_barrier(prediction.astype(jnp.bfloat16))
    multiples = (prediction * panel_len ** (-0.5)).astype(jnp.bfloat16)

    def runs_total(partial_terms):
        return neighbour_sum(partial_terms, src_count, rcv_pos, rcv_count)

    primaries = run_sweeps(record, pred_round, runs_total).astype(jnp.bfloat16)
    return (primaries, multiples)

HALO = 2 * REACH
MESH = pl.DeviceIdType.MESH


def wide_spans(width):
    spans = [(start, 256) for start in range(0, width - 255, 256)]
    done = 256 * (width // 256)
    return spans + ([(done, width - done)] if done < width else [])


def band(shape, shift, period):
    rows = lax.broadcasted_iota(jnp.int32, shape, 0)
    cols = lax.broadcasted_iota(jnp.int32, shape, 1) + shift
    gap = jnp.abs(rows - cols)
    if period:
        gap = jnp.minimum(gap, period - gap)
    return jnp.where(gap <= REACH, 1.0, 0.0).astype(jnp.bfloat16)


def sweep_kernel(
    scale, record_ref, rim_ref, side_ref, pred_ref, prim_ref, mult_ref,
    data, predb, terms, partial, totals, row_band, lane_band
):
    runs_len = record_ref.shape[2]
    src_rows = record_ref.shape[3]
    rows = runs_len + 2 * HALO
    width = src_rows + 128
    f32, bf = jnp.float32, jnp.bfloat16

    @pl.when(pl.program_id(0) == 0)
    def _():
        row_band[...] = band((rows, rows), 0, rows)
        lane_band[...] = band((512, 256), 128, 0)

    for chan in range(2):
        data[chan, :runs_len, :src_rows] = record_ref[0, chan]
        data[chan, runs_len:, :src_rows] = rim_ref[chan, 0]
        data[chan, :, src_rows:] = side_ref[chan, 0]

    def put_terms(at, lanes, err, here, guess):
        weight = 1.5 - jnp.tanh(err[0] * err[0] + err[1] * err[1])
        parts = (
            guess[0] * here[0] + guess[1] * here[1],
            guess[0] * here[1] - guess[1] * here[0],
            guess[0] * guess[0] + guess[1] * guess[1],
        )
        for index, part in enumerate(parts):
            terms[index, at, lanes] = (weight * part).astype(bf)

    def new_err(at, lanes):
        here = [data[chan, at, lanes].astype(f32) for chan in range(2)]
        guess = [predb[chan, at, lanes].astype(f32) for chan in range(2)]
        sums = [totals[pl.ds(index * rows + at.start, at.size), lanes] for index in range(3)]
        inverse = 1.0 / (sums[2] + weight_eps)
        gain_real = sums[0] * inverse
        gain_imag = sums[1] * inverse
        err = (
            here[0] - (gain_real * guess[0] - gain_imag * guess[1]),
            here[1] - (gain_real * guess[1] + gain_imag * guess[0]),
        )
        return err, here, guess

    def box():
        for index in range(3):
            part = slice(index * rows, (index + 1) * rows)
            for start, size in wide_spans(width):
                partial[part, 128 + start : 128 + start + size] = jnp.dot(
                    row_band[...], terms[index, :, start : start + size], preferred_element_type=f32
                ).astype(bf)
        partial[:, :128] = partial[:, width : width + 128]
        partial[:, width + 128 :] = partial[:, 128:256]
        for start, size in wide_spans(width):
            totals[:, start : start + size] = jnp.dot(
                partial[:, start : start + size + 256],
                lane_band[: size + 256, :size],
                preferred_element_type=f32,
            )

    @pl.loop(0, rows // 16)
    def _(step):
        at = pl.ds(pl.multiple_of(step * 16, 16), 16)
        for block in range(width // 128):
            lanes = slice(block * 128, (block + 1) * 128)
            here = [data[chan, at, lanes].astype(f32) for chan in range(2)]
            guess = []
            for chan in range(2):
                rounded = pred_ref[chan, 0, at, lanes].astype(bf)
                predb[chan, at, lanes] = rounded
                guess.append(rounded.astype(f32))
            put_terms(at, lanes, here, here, guess)

    @pl.loop(0, runs_len // 16)
    def _(step):
        at = pl.ds(pl.multiple_of(step * 16, 16), 16)
        for block in range(src_rows // 128):
            lanes = slice(block * 128, (block + 1) * 128)
            for chan in range(2):
                mult_ref[0, chan, at, lanes] = (pred_ref[chan, 0, at, lanes] * scale).astype(bf)

    for sweep_step in range(SWEEPS - 1):
        box()

        @pl.loop(0, rows // 16)
        def _(step):
            at = pl.ds(pl.multiple_of(step * 16, 16), 16)
            for block in range(width // 128):
                lanes = slice(block * 128, (block + 1) * 128)
                put_terms(at, lanes, *new_err(at, lanes))

    box()

    @pl.loop(0, runs_len // 16)
    def _(step):
        at = pl.ds(pl.multiple_of(step * 16, 16), 16)
        for block in range(src_rows // 128):
            lanes = slice(block * 128, (block + 1) * 128)
            err, _, _ = new_err(at, lanes)
            prim_ref[0, 0, at, lanes] = err[0].astype(bf)
            prim_ref[0, 1, at, lanes] = err[1].astype(bf)


def sweep_call(record, rims, sides, pred, panel):
    _, _, rcv_cols, src_rows = record.shape
    _, runs, rows, width = pred.shape
    run_len = rcv_cols // runs
    f32, bf = jnp.float32, jnp.bfloat16
    out = jax.ShapeDtypeStruct(record.shape, bf)
    tile = pl.BlockSpec((1, 2, run_len, src_rows), lambda r: (0, 0, r, 0))
    return pl.pallas_call(
        functools.partial(sweep_kernel, panel ** (-0.5)),
        grid=(runs,),
        out_shape=(out, out),
        in_specs=[
            tile,
            pl.BlockSpec((2, 1, 2 * HALO, src_rows), lambda r: (0, r, 0, 0)),
            pl.BlockSpec((2, 1, rows, 128), lambda r: (0, r, 0, 0)),
            pl.BlockSpec((2, 1, rows, width), lambda r: (0, r, 0, 0)),
        ],
        out_specs=(tile, tile),
        scratch_shapes=[
            pltpu.VMEM((2, rows, width), bf),
            pltpu.VMEM((2, rows, width), bf),
            pltpu.VMEM((3, rows, width), bf),
            pltpu.VMEM((3 * rows, width + 256), bf),
            pltpu.VMEM((3 * rows, width), f32),
            pltpu.VMEM((rows, rows), bf),
            pltpu.VMEM((512, 256), bf),
        ],
        compiler_params=pltpu.CompilerParams(vmem_limit_bytes=56 * 1024 * 1024),
        cost_estimate=pl.CostEstimate(
            flops=12_000_000_000, bytes_accessed=4 * record.size * 2, transcendentals=2 * record.size
        ),
    )(record, rims, sides, pred)


def roll(values, shift):
    return pltpu.roll(values, shift % 128, 1) if shift % 128 else values


def lanes_of(values):
    return lax.broadcasted_iota(jnp.int32, values.shape, 1)


def pack_traces(traces):
    half, quarter = traces.shape[0] // 2, traces.shape[0] // 4
    wide = jnp.where(
        lanes_of(traces[:half]) < 64, traces[:half], roll(traces[half:], 64)
    )
    lane = lanes_of(traces[:quarter])
    rest = jnp.zeros((quarter, 128), traces.dtype)
    for part in range(4):
        moved = roll(traces[part * quarter : (part + 1) * quarter], 32 * part - 64)
        rest = jnp.where(lane // 32 == part, moved, rest)
    return jnp.concatenate([wide, rest], axis=0)


def unpack_traces(packed):
    half = packed.shape[0] * 2 // 3
    wide = jnp.concatenate([packed[:half], roll(packed[:half], 64)], axis=0)
    rest = jnp.concatenate([roll(packed[half:], 64 - 32 * part) for part in range(4)], axis=0)
    lane = lanes_of(wide)
    return jnp.where(lane < 64, wide, jnp.where(lane < 96, rest, jnp.zeros_like(rest)))


def exchange_kernel(
    sizes, rec, offset, pred, rims, sides,
    front_tx, front_rx, behind_tx, behind_rx, head_tx, head_rx, tail_tx, tail_rx,
    first_tx, after_rx, last_tx, before_rx, own, next_rx, prev_rx, picks, left, right, right_all, tiles,
    col_pick, row_pick, gathered,
    front_send, front_recv, behind_send, behind_recv, edge_send, edge_recv,
    right_send, right_recv, line_send, left_recv, pair_send, rim_send, rim_recv, out_sem,
):
    srcs, rcvs = sizes
    src = lax.axis_index("src")
    rcv = lax.axis_index("rcv")
    f32, bf = jnp.float32, jnp.bfloat16
    rcv_cols, src_rows = rec.shape[1:]
    run_len = rcv_cols // srcs
    rows = run_len + 2 * HALO
    width = src_rows + 128
    panel = right.shape[3]
    each = panel // (srcs * rcvs)
    spots = rcvs // 2
    spot, core = rcv // 2, lax.rem(rcv, 2)

    def remote(source, target, send, recv, where):
        return pltpu.make_async_remote_copy(
            src_ref=source, dst_ref=target, send_sem=send, recv_sem=recv,
            device_id=where, device_id_type=MESH,
        )

    rcv_peers = [lax.rem(rcv + step, rcvs) for step in range(1, rcvs)]
    src_peers = [lax.rem(src + step, srcs) for step in range(1, srcs)]
    last_rcv, first_rcv = rcv == rcvs - 1, rcv == 0
    has_next = jnp.logical_not(jnp.logical_and(last_rcv, src == srcs - 1))
    has_prev = jnp.logical_not(jnp.logical_and(first_rcv, src == 0))
    next_dev = (
        jnp.where(last_rcv, jnp.minimum(src + 1, srcs - 1), src), jnp.where(last_rcv, 0, rcv + 1)
    )
    prev_dev = (
        jnp.where(first_rcv, jnp.maximum(src - 1, 0), src), jnp.where(first_rcv, rcvs - 1, rcv - 1)
    )
    far_next = jnp.logical_and(last_rcv, src < srcs - 1)
    far_prev = jnp.logical_and(first_rcv, src > 0)

    left[src_rows:] = jnp.zeros((128, 2 * panel), bf)
    barrier = pltpu.get_barrier_semaphore()
    for peer in rcv_peers:
        pl.semaphore_signal(barrier, inc=1, device_id=(src, peer), device_id_type=MESH)
    for peer in src_peers:
        pl.semaphore_signal(barrier, inc=1, device_id=(peer, rcv), device_id_type=MESH)

    @pl.when(far_next)
    def _():
        pl.semaphore_signal(barrier, inc=1, device_id=next_dev, device_id_type=MESH)

    @pl.when(far_prev)
    def _():
        pl.semaphore_signal(barrier, inc=1, device_id=prev_dev, device_id_type=MESH)

    offsets = jnp.broadcast_to(offset[...].astype(f32).reshape(1, panel), (8, panel)).astype(bf)

    def pick_from(target, count, group_of, cell_of):
        groups = lax.broadcasted_iota(jnp.int32, (panel, count), 0)
        column = lax.broadcasted_iota(jnp.int32, (panel, count), 1)
        chosen = jnp.where(groups == group_of(column), 1.0, 0.0).astype(bf)
        mine = jnp.dot(offsets, chosen, preferred_element_type=f32)[:1].astype(jnp.int32)
        cells = lax.broadcasted_iota(jnp.int32, target.shape, 0)
        column = lax.broadcasted_iota(jnp.int32, (1, count), 1)
        target[...] = jnp.where(cells == cell_of(column) + mine, 1.0, 0.0).astype(bf)

    per_src = rcvs * each
    key = lax.broadcasted_iota(jnp.int32, (128, panel), 0)
    groups = lax.broadcasted_iota(jnp.int32, (128, panel), 1)
    chosen = jnp.where(
        groups == key // each * per_src + each * rcv + key % each, 1.0, 0.0
    ).astype(bf)
    mine = lax.dot_general(
        chosen, offsets, (((1,), (1,)), ((), ())), preferred_element_type=f32
    )[:, :1].astype(jnp.int32)
    cells = lax.broadcasted_iota(jnp.int32, (128, rcv_cols), 1)
    key = lax.broadcasted_iota(jnp.int32, (128, 1), 0)
    cell = key // each * run_len + STRIDE * (key % each) + mine
    cell = jnp.where(key < srcs * each, cell, -1)
    col_pick[...] = jnp.where(cells == cell, 1.0, 0.0).astype(bf)
    pick_from(row_pick, per_src, lambda j: per_src * src + j, lambda j: STRIDE * j)

    for chan in range(2):
        for pair in range(srcs // 2):
            for buffer, start in ((head_tx, 0), (tail_tx, run_len - 16)):
                ends = [
                    rec[chan, run * run_len + start : run * run_len + start + 16].astype(f32)
                    for run in (2 * pair, 2 * pair + 1)
                ]
                part = slice(0, HALO) if start == 0 else slice(16 - HALO, 16)
                buffer[chan, 16 * pair : 16 * pair + 16] = jnp.concatenate(
                    [end[part] for end in ends], axis=0
                ).astype(bf)

    pl.semaphore_wait(
        barrier,
        rcvs - 1 + srcs - 1 + jnp.where(far_next, 1, 0) + jnp.where(far_prev, 1, 0),
    )
    heads = remote(
        head_tx, head_rx, edge_send.at[0], edge_recv.at[0], (src, lax.rem(rcv + rcvs - 1, rcvs))
    )
    tails = remote(tail_tx, tail_rx, edge_send.at[1], edge_recv.at[1], (src, lax.rem(rcv + 1, rcvs)))
    heads.start()
    tails.start()

    fronts, behinds = [], []
    for chan in range(2):
        picked = jnp.transpose(jnp.dot(col_pick[...], rec[chan], preferred_element_type=f32))
        for peer in range(rcvs):
            front_tx[peer, chan] = pack_traces(
                picked[peer * run_len : (peer + 1) * run_len]
            ).astype(bf)
        for index, peer in enumerate(rcv_peers):
            copy = remote(
                front_tx.at[peer, chan], front_rx.at[rcv, chan], front_send.at[chan, index],
                front_recv.at[chan, rcv], (src, peer),
            )
            copy.start()
            fronts.append(copy)
        front_rx[rcv, chan] = front_tx[rcv, chan]
    for chan in range(2):
        picked = jnp.dot(rec[chan], row_pick[...], preferred_element_type=f32).astype(bf)
        for peer in range(srcs):
            behind_tx[peer, chan] = picked[peer * run_len : (peer + 1) * run_len]
        for index, peer in enumerate(src_peers):
            copy = remote(
                behind_tx.at[peer, chan], behind_rx.at[src, chan], behind_send.at[chan, index],
                behind_recv.at[chan, src], (peer, rcv),
            )
            copy.start()
            behinds.append(copy)
        behind_rx[src, chan] = behind_tx[src, chan]

    for peer in range(rcvs):
        index = lax.broadcasted_iota(jnp.int32, (128, panel), 0)
        column = lax.broadcasted_iota(jnp.int32, (128, panel), 1)
        aim = index // each * (rcvs * each) + peer * each + index % each
        picks[peer * 128 : (peer + 1) * 128] = jnp.where(column == aim, 1.0, 0.0).astype(bf)

    heads.wait()
    tails.wait()

    def edge(buffer, chan, run):
        if run < 0 or run >= srcs:
            return jnp.zeros((HALO, src_rows), f32)
        tile = buffer[chan, run // 2 * 16 : run // 2 * 16 + 16].astype(f32)
        return tile[run % 2 * HALO : run % 2 * HALO + HALO]

    packs = [jnp.zeros((rows, 128), f32), jnp.zeros((rows, 128), f32)]
    for chan in range(2):
        for run in range(srcs):
            below = jnp.where(last_rcv, edge(head_rx, chan, run + 1), edge(head_rx, chan, run))
            above = jnp.where(first_rcv, edge(tail_rx, chan, run - 1), edge(tail_rx, chan, run))
            rim = jnp.concatenate([below, above], axis=0).astype(bf)
            rims[chan, run] = rim
            main = slice(run * run_len, (run + 1) * run_len)
            slot = chan * srcs + run
            for block, lanes in enumerate((slice(0, 128), slice(src_rows - 128, src_rows))):
                side = jnp.concatenate(
                    [rec[chan, main, lanes].astype(f32), rim[:, lanes].astype(f32)], axis=0
                )
                moved = roll(side, HALO * slot + HALO * block)
                packs[block] = jnp.where(lanes_of(side) // HALO == slot, moved, packs[block])
    first_tx[...] = packs[0].astype(bf)
    last_tx[...] = packs[1].astype(bf)

    low = jnp.maximum(src - 1, 0)
    high = jnp.minimum(src + 1, srcs - 1)
    firsts = remote(first_tx, after_rx, edge_send.at[2], edge_recv.at[2], (low, rcv))
    lasts = remote(last_tx, before_rx, edge_send.at[3], edge_recv.at[3], (high, rcv))

    @pl.when(src > 0)
    def _():
        firsts.start()

    @pl.when(src < srcs - 1)
    def _():
        lasts.start()

    def line(owner_spot, source, up, step, chan):
        owner = 2 * owner_spot + core
        shift = 2 if up else -2
        return remote(
            source, shard(owner, chan), line_send.at[chan, 0 if up else 1, step],
            left_recv.at[chan, owner], (src, jnp.clip(rcv + shift, 0, rcvs - 1)),
        )

    def hand(owner, source, chan):
        return remote(
            source, shard(owner, chan), pair_send.at[chan, owner // 2], left_recv.at[chan, owner],
            (src, rcv + 1 - 2 * core),
        )

    def shard(owner, chan):
        return left.at[
            pl.ds(pl.multiple_of(owner * run_len, 16), run_len), pl.ds(chan * panel, panel)
        ]

    def right_copy(kind, index, slot, peer):
        rims_only = kind == 2
        at = pl.ds(run_len, 2 * HALO) if rims_only else pl.ds(0, run_len)
        chans = pl.ds(0, 2) if rims_only else pl.ds(kind, 1)
        return remote(
            own.at[chans, at], right.at[slot, chans, at], right_send.at[kind, index],
            right_recv.at[kind, slot], (peer, rcv),
        )

    to_prev, to_next = [], []
    for chan in range(2):
        for index, step in enumerate(range(1, rcvs)):
            peer = lax.rem(rcv + rcvs - step, rcvs)
            remote(
                front_tx.at[peer, chan], front_rx.at[peer, chan], front_send.at[chan, index],
                front_recv.at[chan, peer], (src, peer),
            ).wait_recv()
        for index, step in enumerate(range(1, srcs)):
            peer = lax.rem(src + srcs - step, srcs)
            remote(
                behind_tx.at[peer, chan], behind_rx.at[peer, chan], behind_send.at[chan, index],
                behind_recv.at[chan, peer], (peer, rcv),
            ).wait_recv()
        for peer in range(rcvs):
            gathered[:, peer * 128 : (peer + 1) * 128] = unpack_traces(
                front_rx[peer, chan].astype(f32)
            ).astype(bf)
        total = jnp.dot(gathered[...], picks[...], preferred_element_type=f32)
        for peer in range(srcs):
            shape = (rcvs * each, panel)
            index = lax.broadcasted_iota(jnp.int32, shape, 0)
            column = lax.broadcasted_iota(jnp.int32, shape, 1)
            pick = jnp.where(column == index + peer * rcvs * each, 1.0, 0.0).astype(bf)
            total = total + jnp.dot(behind_rx[peer, chan], pick, preferred_element_type=f32)
        own[chan, :run_len] = (total * 0.5).astype(bf)
        mine = own.at[chan, pl.ds(0, run_len)]

        @pl.when(spot < spots - 1)
        def _():
            line(spot, mine, True, 0, chan).start()

        @pl.when(spot > 0)
        def _():
            line(spot, mine, False, 0, chan).start()

        hand(rcv, mine, chan).start()
        for index, peer in enumerate(src_peers):
            right_copy(chan, index, src, peer).start()
        to_prev.append(
            remote(
                own.at[chan, pl.ds(0, 16)], next_rx.at[chan], edge_send.at[4 + chan],
                edge_recv.at[4 + chan], prev_dev,
            )
        )
        to_next.append(
            remote(
                own.at[chan, pl.ds(run_len - 16, 16)], prev_rx.at[chan], edge_send.at[6 + chan],
                edge_recv.at[6 + chan], next_dev,
            )
        )

        @pl.when(has_prev)
        def _():
            to_prev[chan].start()

        @pl.when(has_next)
        def _():
            to_next[chan].start()

        left[
            pl.ds(pl.multiple_of(rcv * run_len, 16), run_len), chan * panel : (chan + 1) * panel
        ] = own[chan, :run_len]

    @pl.when(has_next)
    def _():
        for chan in range(2):
            to_prev[chan].wait_recv()

    @pl.when(jnp.logical_not(has_next))
    def _():
        next_rx[...] = jnp.zeros_like(next_rx)

    @pl.when(has_prev)
    def _():
        for chan in range(2):
            to_next[chan].wait_recv()

    @pl.when(jnp.logical_not(has_prev))
    def _():
        prev_rx[...] = jnp.zeros_like(prev_rx)

    place = lax.broadcasted_iota(jnp.int32, (2, 2 * HALO, panel), 1)
    own[:, run_len:] = jnp.where(place < HALO, next_rx[...], prev_rx[...])
    for index, peer in enumerate(src_peers):
        right_copy(2, index, src, peer).start()
    right[src] = own[...]

    def rim_copy(start, chan, index, which, peer):
        return remote(
            own.at[chan, pl.ds(run_len, 2 * HALO)],
            left.at[pl.ds(start, 2 * HALO), pl.ds(chan * panel, panel)],
            rim_send.at[chan, index], rim_recv.at[chan, which], (src, peer),
        )

    rim_ends = ((first_rcv, width - 2 * HALO, 0), (last_rcv, src_rows, 1))
    for holds, start, which in rim_ends:

        @pl.when(holds)
        def _():
            for chan in range(2):
                for index, peer in enumerate(rcv_peers):
                    rim_copy(start, chan, index, which, peer).start()
                left[start : start + 2 * HALO, chan * panel : (chan + 1) * panel] = own[
                    chan, run_len:
                ]

    def set_right(run):
        real, imag = right[run, 0], right[run, 1]
        top = slice(run * rows, (run + 1) * rows)
        bottom = slice((srcs + run) * rows, (srcs + run + 1) * rows)
        right_all[top, :panel] = real
        right_all[top, panel:] = -imag
        right_all[bottom, :panel] = imag
        right_all[bottom, panel:] = real

    def multiply(start, size):
        at = pl.ds(start, size)
        tiles[:, :, :, at] = lax.dot_general(
            right_all[...], left[at, :], (((1,), (1,)), ((), ())), preferred_element_type=f32
        ).reshape(2, srcs, rows, size)

    def out_copy(start, size, index):
        return pltpu.make_async_copy(
            tiles.at[:, :, :, pl.ds(start, size)],
            pred.at[:, :, :, pl.ds(start, size)],
            out_sem.at[index],
        )

    span = 2 * run_len

    def tile_of(owner_spot):
        for chan in range(2):
            hand(2 * owner_spot + 1 - core, shard(rcv, chan), chan).wait_recv()
        start = pl.multiple_of(owner_spot * span, 128)
        multiply(start, span)
        out_copy(start, span, owner_spot).start()

    def tiles_when(ready):
        @pl.loop(0, spots)
        def _(other):
            @pl.when(ready(jnp.abs(other - spot)))
            def _():
                tile_of(other)

    for step in range(1, spots):
        if step == spots - 1:
            for other in range(1, srcs):
                peer = lax.rem(src + srcs - other, srcs)
                for kind in range(3):
                    right_copy(kind, 0, peer, peer).wait_recv()
            for run in range(srcs):
                set_right(run)
            tiles_when(lambda gap: gap < spots - 1)
            for holds, start, which in rim_ends:

                @pl.when(jnp.logical_not(holds))
                def _():
                    for chan in range(2):
                        rim_copy(start, chan, 0, which, rcv).wait_recv()

            multiply(src_rows, 128)
            out_copy(src_rows, 128, spots).start()
        for chan in range(2):
            for up in (True, False):
                owner_spot = spot - step if up else spot + step
                arrives = spot >= step if up else spot + step < spots
                onward = spot < spots - 1 if up else spot > 0

                @pl.when(arrives)
                def _():
                    owner = 2 * owner_spot + core
                    block = shard(owner, chan)
                    line(owner_spot, block, up, step - 1, chan).wait_recv()
                    if step < spots - 1:

                        @pl.when(onward)
                        def _():
                            line(owner_spot, block, up, step, chan).start()

                    hand(owner, block, chan).start()

    tiles_when(lambda gap: gap == spots - 1)

    for copy in fronts + behinds:
        copy.wait_send()

    @pl.when(src > 0)
    def _():
        firsts.wait_send()
        lasts.wait_recv()

    @pl.when(src < srcs - 1)
    def _():
        lasts.wait_send()
        firsts.wait_recv()

    @pl.when(src == 0)
    def _():
        before_rx[...] = jnp.zeros_like(before_rx)

    @pl.when(src == srcs - 1)
    def _():
        after_rx[...] = jnp.zeros_like(after_rx)

    after, before = after_rx[...].astype(f32), before_rx[...].astype(f32)
    lane = lanes_of(after)
    zero = jnp.zeros((rows, 128), f32)
    for chan in range(2):
        for run in range(srcs):
            slot = chan * srcs + run
            high_side = jnp.where(lane >= 128 - HALO, roll(before, 128 - HALO - HALO * slot), zero)
            sides[chan, run] = jnp.where(
                lane < HALO, roll(after, -HALO * slot), high_side
            ).astype(bf)

    for chan in range(2):

        @pl.when(has_prev)
        def _():
            to_prev[chan].wait_send()

        @pl.when(has_next)
        def _():
            to_next[chan].wait_send()

        for holds, start, which in rim_ends:

            @pl.when(holds)
            def _():
                for index, peer in enumerate(rcv_peers):
                    rim_copy(start, chan, index, which, peer).wait_send()

        mine = own.at[chan, pl.ds(0, run_len)]
        for step in range(spots - 1):

            @pl.when(jnp.logical_and(spot < spots - 1, spot >= step))
            def _():
                line(spot, mine, True, step, chan).wait_send()

            @pl.when(jnp.logical_and(spot > 0, spot + step < spots))
            def _():
                line(spot, mine, False, step, chan).wait_send()

        for index in range(spots):
            hand(2 * index + core, mine, chan).wait_send()

    for kind in range(3):
        for index, peer in enumerate(src_peers):
            right_copy(kind, index, src, peer).wait_send()
    for index in range(spots):
        out_copy(index * span, span, index).wait()
    out_copy(src_rows, 128, spots).wait()


def exchange_call(rec, panel_offset, srcs, rcvs):
    _, rcv_cols, src_rows = rec.shape
    run_len = rcv_cols // srcs
    rows = run_len + 2 * HALO
    panel = panel_offset.shape[0]
    each = panel // (srcs * rcvs)
    bf = jnp.bfloat16
    vmem = pl.BlockSpec(memory_space=pltpu.VMEM)
    front = (rcvs, 2, run_len * 3 // 4, 128)
    behind = (srcs, 2, run_len, rcvs * each)
    edges = (2, HALO * srcs, src_rows)
    side = (2, srcs, rows, 128)
    pack = (rows, 128)
    shapes = [front, front, behind, behind, edges, edges, edges, edges, pack, pack, pack, pack]
    shapes += [(2, rows, panel), (2, 16, panel), (2, 16, panel), (rcvs * 128, panel)]
    shapes += [(src_rows + 128, 2 * panel), (srcs, 2, rows, panel), (2 * srcs * rows, 2 * panel)]
    wide = (2, srcs, rows, src_rows + 128)
    dma = pltpu.SemaphoreType.DMA
    return pl.pallas_call(
        functools.partial(exchange_kernel, (srcs, rcvs)),
        out_shape=(
            jax.ShapeDtypeStruct(wide, jnp.float32),
            jax.ShapeDtypeStruct((2, srcs, 2 * HALO, src_rows), bf),
            jax.ShapeDtypeStruct(side, bf),
        ),
        in_specs=[vmem] * 2,
        out_specs=(pl.BlockSpec(memory_space=pl.ANY), vmem, vmem),
        scratch_shapes=[pltpu.VMEM(shape, bf) for shape in shapes]
        + [
            pltpu.VMEM(wide, jnp.float32),
            pltpu.VMEM((128, rcv_cols), bf),
            pltpu.VMEM((src_rows, rcvs * each), bf),
            pltpu.VMEM((run_len, rcvs * 128), bf),
        ]
        + [
            dma((2, rcvs)), dma((2, rcvs)), dma((2, srcs)), dma((2, srcs)), dma((8,)), dma((8,)),
            dma((3, srcs)), dma((3, srcs)), dma((2, 2, rcvs // 2)), dma((2, rcvs)), dma((2, rcvs // 2)),
            dma((2, rcvs)), dma((2, 2)), dma((rcvs // 2 + 1,)),
        ],
        compiler_params=pltpu.CompilerParams(
            collective_id=0, has_side_effects=True, vmem_limit_bytes=56 * 1024 * 1024
        ),
        cost_estimate=pl.CostEstimate(
            flops=10_000_000_000, bytes_accessed=8 * rec.size, transcendentals=0
        ),
    )(rec, panel_offset)


def shards(record, panel_offset):
    src_count = lax.axis_size("src")
    rcv_count = lax.axis_size("rcv")
    freqs, _, rcv_cols, src_rows = record.shape
    run_len = rcv_cols // src_count
    if freqs != 1 or run_len % 16 or src_rows % 128 or src_count % 2 or rcv_count % 2 or run_len % 64 or rcv_count < 4 or src_count * run_len > 96 * STRIDE or src_count * HALO > 64:
        return plain_shards(record, panel_offset)
    pred, rims, sides = exchange_call(record[0], panel_offset, src_count, rcv_count)
    return sweep_call(record, rims, sides, pred, panel_offset.shape[0])


def solution(mesh):
    in_specs = (P(None, None, "rcv", "src"), P())
    out_specs = (P(None, None, "rcv", "src"), P(None, None, "rcv", "src"))
    return jax.shard_map(shards, mesh=mesh, in_specs=in_specs, out_specs=out_specs, check_vma=False)
```
